256 devices in a mesh: dep: 32 (over y, x, z_hi), hgt: 8 (over z_lo, core).
Axes of the slice: x: 4, y: 4, z: 8 (z_hi: 2, z_lo: 4; z = z_hi * 4 + z_lo), core: 2. Of those that a mesh axis runs over, the one named last changes fastest.
Arguments:
- volume: bfloat16 [64, 64, 64, 512], P('dep', 'hgt'), may hold values from -30 to 30
- qkv_weight: bfloat16 [3, 512, 1536], replicated, may hold values from -2 to 2
- out_weight: bfloat16 [3, 512, 512], replicated, may hold values from -0.25 to 0.25
- norm_gain: float32 [4, 512], replicated, may hold values from 0.1 to 1.9
- up_weight: bfloat16 [512, 2048], replicated, may hold values from -0.25 to 0.25
- down_weight: bfloat16 [2048, 512], replicated, may hold values from -0.125 to 0.125
Outputs:
- result_volume: bfloat16 [64, 64, 64, 512], P('dep', 'hgt')
The draws below stay inside these ranges and needn't reach their ends.
All inputs are finite; a program needn't handle non-finite values.
Results may differ from the reference program's by a relative error of at most 0.024.
Values may be sent and summed in bfloat16 or wider, within the bound.
No kernel may reach another device: no remote copies, remote signals or barrier semaphores. Data moves between devices by JAX's collectives and lax.ppermute only.
A program may use at most 128 MiB of HBM per device.

```python
import math
import jax
import jax.numpy as jnp
from jax import lax

D = 512
HEADS = 8
FF = 2048
NW = 64
NZ = 64
NH = 64


def draw_volume(key, part):
    key = jax.random.fold_in(key, 1)
    sample = jnp.clip(jax.random.normal(key, (NZ, NH, NW, D), jnp.float32), -6.0, 6.0)
    return sample.astype(jnp.bfloat16)


def draw_qkv_weight(key, part):
    key = jax.random.fold_in(key, 2)
    weights = jnp.clip(jax.random.normal(key, (3, D, 3 * D), jnp.float32), -6.0, 6.0) * (1.0 / math.sqrt(D))
    return weights.astype(jnp.bfloat16)


def scatter_about(own_key, dims, scale, limit, kind=jnp.bfloat16):
    return jnp.clip(scale * jax.random.normal(own_key, dims, jnp.float32), -limit, limit).astype(kind)


def setup_inputs(seed: int = 0) -> dict:
    streams_of = jax.random.split(jax.random.key(seed), 7)
    return {
        "volume": draw_volume(jax.random.fold_in(streams_of[6], 71), 0),
        "qkv_weight": draw_qkv_weight(jax.random.fold_in(streams_of[6], 71), 0),
        "out_weight": scatter_about(streams_of[2], (3, D, D), D ** -0.5, 0.25),
        "norm_gain": jnp.clip(1.0 + 0.18 * jax.random.normal(streams_of[3], (4, D), jnp.float32), 0.1, 1.9),
        "up_weight": scatter_about(streams_of[4], (D, FF), D ** -0.5, 0.25),
        "down_weight": scatter_about(streams_of[5], (FF, D), FF ** -0.5, 0.125),
    }


epsilon = 1e-05

def layer_norm(values, gain_row):
    widened = values.astype(jnp.float32)
    center = lax.optimization_barrier(jnp.mean(widened, axis=-1, keepdims=True))
    shifted = widened - center
    spread = lax.optimization_barrier(jnp.mean(shifted * shifted, axis=-1, keepdims=True))
    return shifted * lax.rsqrt(spread + epsilon) * gain_row

def flat_product(left, weight):
    leading = left.shape[:-1]
    product = jnp.dot(left.reshape(-1, left.shape[-1]), weight, preferred_element_type=jnp.float32)
    return product.reshape(leading + (weight.shape[1],))

def attend_lines(queries, key_part, value_part):
    outer, length, inner, features = queries.shape
    head_size = features // HEADS
    queries_h = queries.astype(jnp.float32).reshape(outer, length, inner, HEADS, head_size)
    keys_h = key_part.astype(jnp.float32).reshape(outer, key_part.shape[1], inner, HEADS, head_size)
    values_h = value_part.astype(jnp.float32).reshape(outer, value_part.shape[1], inner, HEADS, head_size)
    scores = jnp.einsum('albhe,ambhe->abhlm', queries_h, keys_h) * (1.0 / math.sqrt(head_size))
    attention = jax.nn.softmax(scores, axis=-1).astype(jnp.bfloat16)
    mixed = jnp.einsum('abhlm,ambhe->albhe', attention.astype(jnp.float32), values_h)
    return mixed.astype(jnp.bfloat16).reshape(outer, length, inner, features)

def axial_block(tokens4, gain_row, qkv_part, out_part):
    normed = layer_norm(tokens4, gain_row).astype(jnp.bfloat16)
    projected = flat_product(normed, qkv_part).astype(jnp.bfloat16)
    mixed = attend_lines(projected[..., :D], projected[..., D:2 * D], projected[..., 2 * D:])
    return (tokens4.astype(jnp.float32) + flat_product(mixed, out_part)).astype(jnp.bfloat16)

def feed_forward(tokens, gain_row, up_weight, down_weight):
    normed = layer_norm(tokens, gain_row).astype(jnp.bfloat16)
    hidden = jax.nn.gelu(flat_product(normed, up_weight)).astype(jnp.bfloat16)
    return (tokens.astype(jnp.float32) + flat_product(hidden, down_weight)).astype(jnp.bfloat16)

def reference(volume, qkv_weight, out_weight, norm_gain, up_weight, down_weight):

    def width_slab(depth_slab):
        lines = axial_block(depth_slab.reshape(NH, NW, 1, D), norm_gain[0], qkv_weight[0], out_weight[0])
        return lines.reshape(NH, NW, D)
    current = lax.map(width_slab, volume)

    def height_slab(depth_slab):
        return axial_block(depth_slab[None], norm_gain[1], qkv_weight[1], out_weight[1])[0]
    current = lax.map(height_slab, current)
    turned = jnp.swapaxes(current, 0, 1)

    def depth_slab_pass(height_slab_in):
        attended = axial_block(height_slab_in[None], norm_gain[2], qkv_weight[2], out_weight[2])[0]
        return feed_forward(attended, norm_gain[3], up_weight, down_weight)
    turned = lax.map(depth_slab_pass, turned)
    return jnp.swapaxes(turned, 0, 1)
```

```python
import functools

import jax
import jax.numpy as jnp
from jax import lax
from jax.experimental import pallas as pl
from jax.experimental.pallas import tpu as pltpu
from jax.sharding import Mesh
from jax.sharding import PartitionSpec as P

D = 512
HEADS = 8
HEAD = 64
FF = 2048
LINE = 64
GROUP = 4
ROWS = GROUP * LINE
TOKENS = 1024
EPS = 1e-5
F32 = jnp.float32
BF16 = jnp.bfloat16


def layer_norm(x, gain):
    center = jnp.mean(x, axis=-1, keepdims=True)
    shifted = x - center
    spread = jnp.mean(shifted * shifted, axis=-1, keepdims=True)
    return (shifted * lax.rsqrt(spread + EPS) * gain).astype(BF16)


def attend(x, gain, qkv_ref, out_ref, ones_ref):
    normed = layer_norm(x, gain)
    q = jnp.dot(normed, qkv_ref[:, :D], preferred_element_type=F32)
    q = (q * (HEAD**-0.5)).astype(BF16)
    k = jnp.dot(normed, qkv_ref[:, D : 2 * D], preferred_element_type=F32).astype(BF16)
    v = jnp.dot(normed, qkv_ref[:, 2 * D :], preferred_element_type=F32).astype(BF16)
    wide = 4 * HEAD
    lane_head = lax.broadcasted_iota(jnp.int32, (LINE, wide), 1) // HEAD
    low = lax.broadcasted_iota(jnp.int32, (LINE, 128), 1) < HEAD
    zero = jnp.zeros((LINE, wide), BF16)
    halves = []
    for g in range(2):
        cols = slice(g * wide, (g + 1) * wide)
        exps = []
        mixed = []
        for line in range(GROUP):
            rows = slice(line * LINE, (line + 1) * LINE)
            kk, vv = k[rows, cols], v[rows, cols]
            k_diag = jnp.concatenate(
                [jnp.where(lane_head == h, kk, zero) for h in range(4)], axis=0
            )
            v_diag = jnp.concatenate(
                [jnp.where(lane_head == h, vv, zero) for h in range(4)], axis=0
            )
            scores = lax.dot_general(
                q[rows, cols], k_diag, (((1,), (1,)), ((), ())), preferred_element_type=F32
            )
            parts = []
            for half in range(2):
                s = scores[:, half * 128 : (half + 1) * 128]
                top_low = jnp.max(jnp.where(low, s, -jnp.inf), axis=-1, keepdims=True)
                top_high = jnp.max(jnp.where(low, -jnp.inf, s), axis=-1, keepdims=True)
                parts.append(jnp.exp(s - jnp.where(low, top_low, top_high)).astype(BF16))
            e = jnp.concatenate(parts, axis=1)
            exps.append(e)
            mixed.append(jnp.dot(e, v_diag, preferred_element_type=F32))
        sums = jnp.dot(
            jnp.concatenate(exps, axis=0), ones_ref[...], preferred_element_type=F32
        )
        halves.append((jnp.concatenate(mixed, axis=0) / sums).astype(BF16))
    attended = jnp.concatenate(halves, axis=1)
    return x + jnp.dot(attended, out_ref[...], preferred_element_type=F32)


def width_kernel(x_ref, gain_ref, qkv_ref, out_w_ref, ones_ref, y_ref):
    x = x_ref[...].reshape(ROWS, D).astype(F32)
    y = attend(x, gain_ref[0:1, :], qkv_ref, out_w_ref, ones_ref)
    for z in range(8):
        pieces = [y[h * LINE + 8 * z : h * LINE + 8 * z + 8, :] for h in range(GROUP)]
        y_ref[z, 0] = jnp.concatenate(pieces, axis=0).astype(BF16)


def spread(x_ref, xs):
    for c in range(4):
        xs[c] = x_ref[:, c * 128 : (c + 1) * 128].astype(F32)


def gather(ys, y_ref):
    for c in range(4):
        y_ref[:, c * 128 : (c + 1) * 128] = ys[c].astype(BF16)


def take(xs, start, count, stride):
    return jnp.concatenate([xs[c, pl.ds(start, count, stride=stride), :] for c in range(4)], axis=1)


def put(ys, start, count, stride, value):
    for c in range(4):
        ys[c, pl.ds(start, count, stride=stride), :] = value[:, c * 128 : (c + 1) * 128]


def height_kernel(x_ref, gain_ref, qkv_ref, out_w_ref, ones_ref, y_ref, xs, ys):
    spread(x_ref, xs)

    def step(i, carry):
        zh, wsub = i // 2, i % 2
        x = jnp.concatenate(
            [take(xs, zh * 512 + wsub * 4 + w4, LINE, 8) for w4 in range(4)], axis=0
        )
        y = attend(x, gain_ref[1:2, :], qkv_ref, out_w_ref, ones_ref)
        for w4 in range(4):
            for zl in range(4):
                for c in range(2):
                    at = w4 * LINE + (zl * 2 + c) * 8
                    start = wsub * 64 + c * 32 + zl * 8 + zh * 4 + w4
                    put(ys, start, 8, 128, y[at : at + 8, :])
        return carry

    lax.fori_loop(0, 4, step, 0)
    gather(ys, y_ref)


def depth_kernel(x_ref, gain_ref, qkv_ref, out_w_ref, ones_ref, up_ref, down_ref, y_ref, xs, ys):
    spread(x_ref, xs)

    def step(zl, carry):
        x = jnp.concatenate(
            [
                take(xs, d0 * 32 + zl * 8 + zh * 4 + w4, 16, 64)
                for w4 in range(4)
                for zh in range(2)
                for d0 in range(2)
            ],
            axis=0,
        )
        x = attend(x, gain_ref[2:3, :], qkv_ref, out_w_ref, ones_ref)
        x = x.astype(BF16).astype(F32)
        normed = layer_norm(x, gain_ref[3:4, :])
        total = x
        for part in range(4):
            cols = slice(part * 512, (part + 1) * 512)
            hidden = jnp.dot(normed, up_ref[:, cols], preferred_element_type=F32)
            hidden = jax.nn.gelu(hidden).astype(BF16)
            total = total + jnp.dot(hidden, down_ref[cols, :], preferred_element_type=F32)
        for w4 in range(4):
            for zh in range(2):
                for d0 in range(2):
                    at = w4 * LINE + (zh * 2 + d0) * 16
                    start = zh * 32 + zl * 8 + d0 * 4 + w4
                    put(ys, start, 16, 64, total[at : at + 16, :])
        return carry

    lax.fori_loop(0, 4, step, 0)
    gather(ys, y_ref)


def place_kernel(x_ref, y_ref):
    low = lax.broadcasted_iota(jnp.int32, (LINE, D), 0) % 8 < 4
    first = x_ref[0, 0].astype(F32)
    second = x_ref[0, 1].astype(F32)
    y_ref[0, 0] = jnp.where(low, first, pltpu.roll(second, 4, 0)).astype(BF16)
    y_ref[1, 0] = jnp.where(low, pltpu.roll(first, LINE - 4, 0), second).astype(BF16)


PARAMS = pltpu.CompilerParams(vmem_limit_bytes=40 * 1024 * 1024)


def ones_block():
    head = jnp.arange(4 * HEAD) // HEAD
    return (head[:, None] == head[None, :]).astype(BF16)


def weight_specs(layer):
    return [
        pl.BlockSpec((4, D), lambda *i: (0, 0)),
        pl.BlockSpec((None, D, 3 * D), lambda *i: (layer, 0, 0)),
        pl.BlockSpec((None, D, D), lambda *i: (layer, 0, 0)),
        pl.BlockSpec((4 * HEAD, 4 * HEAD), lambda *i: (0, 0)),
    ]


def whole(*shape):
    return pl.BlockSpec(shape, lambda *i: (0,) * len(shape))


def body(volume, qkv_weight, out_weight, norm_gain, up_weight, down_weight):
    ones = ones_block()
    weights = (norm_gain, qkv_weight, out_weight, ones)
    sent = pl.pallas_call(
        width_kernel,
        grid=(4,),
        in_specs=[pl.BlockSpec((1, 4, LINE, D), lambda i: (i // 2, i % 2, 0, 0))] + weight_specs(0),
        out_specs=pl.BlockSpec((8, 1, 32, D), lambda i: (0, i // 2, i % 2, 0)),
        out_shape=jax.ShapeDtypeStruct((8, 2, 64, D), BF16),
        compiler_params=PARAMS,
        name="width",
    )(volume, *weights)
    sent = sent.reshape(16, 64, D)
    held = lax.all_to_all(sent, ("zh", "zl", "c"), split_axis=0, concat_axis=0, tiled=True)
    scratch = [pltpu.VMEM((4, TOKENS, 128), F32), pltpu.VMEM((4, TOKENS, 128), F32)]
    sent = pl.pallas_call(
        height_kernel,
        grid=(1,),
        in_specs=[whole(TOKENS, D)] + weight_specs(1),
        out_specs=whole(TOKENS, D),
        out_shape=jax.ShapeDtypeStruct((TOKENS, D), BF16),
        scratch_shapes=scratch,
        compiler_params=PARAMS,
        name="height",
    )(held.reshape(TOKENS, D), *weights)
    sent = sent.reshape(32, 32, D)
    held = lax.all_to_all(sent, ("y", "x", "c"), split_axis=0, concat_axis=0, tiled=True)
    sent = pl.pallas_call(
        depth_kernel,
        grid=(1,),
        in_specs=[whole(TOKENS, D)] + weight_specs(2) + [whole(D, FF), whole(FF, D)],
        out_specs=whole(TOKENS, D),
        out_shape=jax.ShapeDtypeStruct((TOKENS, D), BF16),
        scratch_shapes=scratch,
        compiler_params=PARAMS,
        name="depth",
    )(held.reshape(TOKENS, D), *weights, up_weight, down_weight)
    sent = sent.reshape(128, 8, D)
    held = lax.all_to_all(sent, ("y", "x", "zh", "zl"), split_axis=0, concat_axis=0, tiled=True)
    return pl.pallas_call(
        place_kernel,
        grid=(8,),
        in_specs=[pl.BlockSpec((1, 2, LINE, D), lambda i: (i, 0, 0, 0))],
        out_specs=pl.BlockSpec((2, 1, LINE, D), lambda i: (0, i, 0, 0)),
        out_shape=jax.ShapeDtypeStruct((2, 8, LINE, D), BF16),
        compiler_params=PARAMS,
        name="place",
    )(held.reshape(8, 2, LINE, D))


def solution(mesh):
    fine = Mesh(mesh.devices.reshape(4, 4, 2, 4, 2), ("y", "x", "zh", "zl", "c"))
    return jax.shard_map(
        body,
        mesh=fine,
        in_specs=(P(("y", "x", "zh"), ("zl", "c"), None, None), P(), P(), P(), P(), P()),
        out_specs=P(("y", "x", "zh"), ("zl", "c"), None, None),
        check_vma=False,
    )
```

```python
import functools

import jax
import jax.numpy as jnp
from jax import lax
from jax.experimental import pallas as pl
from jax.experimental.pallas import tpu as pltpu
from jax.sharding import Mesh
from jax.sharding import PartitionSpec as P

D = 512
HEADS = 8
HEAD = 64
FF = 2048
LINE = 64
TOKENS = 1024
EPS = 1e-5
F32 = jnp.float32
BF16 = jnp.bfloat16


def layer_norm(x, gain):
    center = jnp.mean(x, axis=-1, keepdims=True)
    shifted = x - center
    spread = jnp.mean(shifted * shifted, axis=-1, keepdims=True)
    return (shifted * lax.rsqrt(spread + EPS) * gain).astype(BF16)


def dot(a, b):
    return jnp.dot(a, b, preferred_element_type=F32)


def softmax_top(scores, low):
    parts = []
    for half in range(2):
        s = scores[:, half * 128 : (half + 1) * 128]
        top_low = jnp.max(jnp.where(low, s, -jnp.inf), axis=-1, keepdims=True)
        top_high = jnp.max(jnp.where(low, -jnp.inf, s), axis=-1, keepdims=True)
        parts.append(jnp.exp(s - jnp.where(low, top_low, top_high)).astype(BF16))
    return jnp.concatenate(parts, axis=1)


def attend(x, gain, qkv_ref, out_ref, ones_ref):
    n = x.shape[0] // LINE
    normed = layer_norm(x, gain)
    q = (dot(normed, qkv_ref[:, :D]) * (HEAD**-0.5)).astype(BF16)
    k = dot(normed, qkv_ref[:, D : 2 * D]).astype(BF16).T
    v = dot(normed, qkv_ref[:, 2 * D :]).astype(BF16)
    low_row = lax.broadcasted_iota(jnp.int32, (1, 128), 1) < HEAD
    even = jnp.where(low_row, 1.0, 0.0).astype(BF16)
    odd = jnp.where(low_row, 0.0, 1.0).astype(BF16)
    low = lax.broadcasted_iota(jnp.int32, (LINE, 128), 1) < HEAD
    wide_low = lax.broadcasted_iota(jnp.int32, (LINE, 256), 1) % 128 < HEAD
    zero = jnp.zeros((128, 128), BF16)

    def diagonal(a, b):
        return jnp.concatenate(
            [jnp.concatenate([a, zero], axis=1), jnp.concatenate([zero, b], axis=1)], axis=0
        )

    exps = [[], []]
    mixed = [[], []]
    for pair in range(n // 2):
        at = 128 * pair
        a, b = slice(at, at + LINE), slice(at + LINE, at + 128)
        cells = []
        for p in range(4):
            c = slice(128 * p, 128 * p + 128)
            top = k[128 * p : 128 * p + 64, at : at + 128]
            bottom = k[128 * p + 64 : 128 * p + 128, at : at + 128]
            cells.append(
                (
                    (
                        q[a, c] * even + q[b, c] * odd,
                        jnp.concatenate([top * even, bottom * odd], axis=0),
                        jnp.concatenate([v[a, c] * even, v[b, c] * odd], axis=0),
                    ),
                    (
                        q[b, c] * even + q[a, c] * odd,
                        jnp.concatenate([top * odd, bottom * even], axis=0),
                        jnp.concatenate([v[a, c] * odd, v[b, c] * even], axis=0),
                    ),
                )
            )
        for g in range(2):
            for i in range(2):
                first, second = cells[2 * g][i], cells[2 * g + 1][i]
                scores = dot(
                    jnp.concatenate([first[0], second[0]], axis=1), diagonal(first[1], second[1])
                )
                e = softmax_top(scores, low)
                exps[i].append(e)
                mixed[i].append(dot(e, diagonal(first[2], second[2])))
    sums = [dot(jnp.concatenate(exps[i], axis=0), ones_ref[i]) for i in range(2)]
    rows = []
    for pair in range(n // 2):
        of_a, of_b = [], []
        for g in range(2):
            at = 2 * pair + g
            r = [mixed[i][at] / sums[i][at * LINE : (at + 1) * LINE] for i in range(2)]
            of_a.append(jnp.where(wide_low, r[0], r[1]).astype(BF16))
            of_b.append(jnp.where(wide_low, r[1], r[0]).astype(BF16))
        rows += [jnp.concatenate(of_a, axis=1), jnp.concatenate(of_b, axis=1)]
    return x + dot(jnp.concatenate(rows, axis=0), out_ref[...])


def width_kernel(x_ref, gain_ref, qkv_ref, out_w_ref, ones_ref, y_ref):
    x = x_ref[...].reshape(TOKENS, D).astype(F32)
    y = attend(x, gain_ref[0:1, :], qkv_ref, out_w_ref, ones_ref)
    for d in range(2):
        for z in range(8):
            pieces = [y[(d * 8 + h) * LINE + 8 * z :][:8] for h in range(8)]
            y_ref[z, d] = jnp.concatenate(pieces, axis=0).astype(BF16)


def spread(x_ref, xs):
    for c in range(4):
        xs[c] = x_ref[:, c * 128 : (c + 1) * 128].astype(F32)


def gather(ys, y_ref):
    for c in range(4):
        y_ref[:, c * 128 : (c + 1) * 128] = ys[c].astype(BF16)


def take(xs, start, count, stride):
    return jnp.concatenate([xs[c, pl.ds(start, count, stride=stride), :] for c in range(4)], axis=1)


def put(ys, start, count, stride, value):
    for c in range(4):
        ys[c, pl.ds(start, count, stride=stride), :] = value[:, c * 128 : (c + 1) * 128]


def height_kernel(x_ref, gain_ref, qkv_ref, out_w_ref, ones_ref, y_ref, xs, ys):
    spread(x_ref, xs)
    lines = [(zh, w) for zh in range(2) for w in range(8)]
    x = jnp.concatenate([take(xs, zh * 512 + w, LINE, 8) for zh, w in lines], axis=0)
    y = attend(x, gain_ref[1:2, :], qkv_ref, out_w_ref, ones_ref)
    for n, (zh, w) in enumerate(lines):
        for zl in range(4):
            for c in range(2):
                start = (w // 4) * 64 + c * 32 + zl * 8 + zh * 4 + w % 4
                put(ys, start, 8, 128, y[n * LINE + (zl * 2 + c) * 8 :][:8])
    gather(ys, y_ref)


def depth_kernel(x_ref, gain_ref, qkv_ref, out_w_ref, ones_ref, up_ref, down_ref, y_ref, xs, ys):
    spread(x_ref, xs)
    lines = [(zl, w4) for zl in range(4) for w4 in range(4)]
    quarters = [(zh, d0) for zh in range(2) for d0 in range(2)]
    x = jnp.concatenate(
        [
            take(xs, d0 * 32 + zl * 8 + zh * 4 + w4, 16, 64)
            for zl, w4 in lines
            for zh, d0 in quarters
        ],
        axis=0,
    )
    x = attend(x, gain_ref[2:3, :], qkv_ref, out_w_ref, ones_ref)
    x = x.astype(BF16).astype(F32)
    normed = layer_norm(x, gain_ref[3:4, :])
    total = x
    for part in range(4):
        cols = slice(part * 512, (part + 1) * 512)
        hidden = jax.nn.gelu(dot(normed, up_ref[:, cols])).astype(BF16)
        total = total + dot(hidden, down_ref[cols, :])
    for n, (zl, w4) in enumerate(lines):
        for m, (zh, d0) in enumerate(quarters):
            put(ys, zh * 32 + zl * 8 + d0 * 4 + w4, 16, 64, total[n * LINE + m * 16 :][:16])
    gather(ys, y_ref)


def place_kernel(x_ref, y_ref):
    low = lax.broadcasted_iota(jnp.int32, (LINE, D), 0) % 8 < 4
    for hs in range(8):
        first = x_ref[hs, 0].astype(F32)
        second = x_ref[hs, 1].astype(F32)
        y_ref[0, hs] = jnp.where(low, first, pltpu.roll(second, 4, 0)).astype(BF16)
        y_ref[1, hs] = jnp.where(low, pltpu.roll(first, LINE - 4, 0), second).astype(BF16)


PARAMS = pltpu.CompilerParams(vmem_limit_bytes=40 * 1024 * 1024)


def ones_block():
    head = jnp.arange(4 * HEAD) // HEAD
    straight = head[:, None] == head[None, :]
    crossed = head[:, None] == head[None, :] + 1 - 2 * (head[None, :] % 2)
    return jnp.stack([straight, crossed]).astype(BF16)


def weight_specs(layer):
    return [
        pl.BlockSpec((4, D), lambda *i: (0, 0)),
        pl.BlockSpec((None, D, 3 * D), lambda *i: (layer, 0, 0)),
        pl.BlockSpec((None, D, D), lambda *i: (layer, 0, 0)),
        pl.BlockSpec((2, 4 * HEAD, 4 * HEAD), lambda *i: (0, 0, 0)),
    ]


def whole(*shape):
    return pl.BlockSpec(shape, lambda *i: (0,) * len(shape))


def body(volume, qkv_weight, out_weight, norm_gain, up_weight, down_weight):
    ones = ones_block()
    weights = (norm_gain, qkv_weight, out_weight, ones)
    sent = pl.pallas_call(
        width_kernel,
        grid=(1,),
        in_specs=[whole(2, 8, LINE, D)] + weight_specs(0),
        out_specs=whole(8, 2, 64, D),
        out_shape=jax.ShapeDtypeStruct((8, 2, 64, D), BF16),
        compiler_params=PARAMS,
        name="width",
    )(volume, *weights)
    sent = sent.reshape(16, 64, D)
    held = lax.all_to_all(sent, ("zh", "zl", "c"), split_axis=0, concat_axis=0, tiled=True)
    scratch = [pltpu.VMEM((4, TOKENS, 128), F32), pltpu.VMEM((4, TOKENS, 128), F32)]
    sent = pl.pallas_call(
        height_kernel,
        grid=(1,),
        in_specs=[whole(TOKENS, D)] + weight_specs(1),
        out_specs=whole(TOKENS, D),
        out_shape=jax.ShapeDtypeStruct((TOKENS, D), BF16),
        scratch_shapes=scratch,
        compiler_params=PARAMS,
        name="height",
    )(held.reshape(TOKENS, D), *weights)
    sent = sent.reshape(32, 32, D)
    held = lax.all_to_all(sent, ("y", "x", "c"), split_axis=0, concat_axis=0, tiled=True)
    sent = pl.pallas_call(
        depth_kernel,
        grid=(1,),
        in_specs=[whole(TOKENS, D)] + weight_specs(2) + [whole(D, FF), whole(FF, D)],
        out_specs=whole(TOKENS, D),
        out_shape=jax.ShapeDtypeStruct((TOKENS, D), BF16),
        scratch_shapes=scratch,
        compiler_params=PARAMS,
        name="depth",
    )(held.reshape(TOKENS, D), *weights, up_weight, down_weight)
    sent = sent.reshape(128, 8, D)
    held = lax.all_to_all(sent, ("y", "x", "zh", "zl"), split_axis=0, concat_axis=0, tiled=True)
    return pl.pallas_call(
        place_kernel,
        grid=(1,),
        in_specs=[whole(8, 2, LINE, D)],
        out_specs=whole(2, 8, LINE, D),
        out_shape=jax.ShapeDtypeStruct((2, 8, LINE, D), BF16),
        compiler_params=PARAMS,
        name="place",
    )(held.reshape(8, 2, LINE, D))


def solution(mesh):
    fine = Mesh(mesh.devices.reshape(4, 4, 2, 4, 2), ("y", "x", "zh", "zl", "c"))
    return jax.shard_map(
        body,
        mesh=fine,
        in_specs=(P(("y", "x", "zh"), ("zl", "c"), None, None), P(), P(), P(), P(), P()),
        out_specs=P(("y", "x", "zh"), ("zl", "c"), None, None),
        check_vma=False,
    )
```

```python
import jax
import jax.numpy as jnp
from jax import lax
from jax.experimental import pallas as pl
from jax.experimental.pallas import tpu as pltpu
from jax.sharding import Mesh
from jax.sharding import PartitionSpec as P

D = 512
HEADS = 8
HEAD = 64
FF = 2048
LINE = 64
TOKENS = 1024
EPS = 1e-5
F32 = jnp.float32
BF16 = jnp.bfloat16


def layer_norm(x, gain):
    center = jnp.mean(x, axis=-1, keepdims=True)
    shifted = x - center
    spread = jnp.mean(shifted * shifted, axis=-1, keepdims=True)
    return (shifted * lax.rsqrt(spread + EPS) * gain).astype(BF16)


def dot(a, b):
    return jnp.dot(a, b, preferred_element_type=F32)


def softmax_top(scores, low):
    parts = []
    for half in range(2):
        s = scores[:, half * 128 : (half + 1) * 128]
        top_low = jnp.max(jnp.where(low, s, -jnp.inf), axis=-1, keepdims=True)
        top_high = jnp.max(jnp.where(low, -jnp.inf, s), axis=-1, keepdims=True)
        parts.append(jnp.exp(s - jnp.where(low, top_low, top_high)).astype(BF16))
    return jnp.concatenate(parts, axis=1)


def ones_block(crossed):
    row = lax.broadcasted_iota(jnp.int32, (256, 256), 0) // HEAD
    column = lax.broadcasted_iota(jnp.int32, (256, 256), 1) // HEAD
    if crossed:
        column = column + 1 - 2 * (column % 2)
    return jnp.where(row == column, 1.0, 0.0).astype(BF16)


def attend(x, gain, qkv_ref, out_ref):
    n = x.shape[0] // LINE
    normed = layer_norm(x, gain)
    q = (dot(normed, qkv_ref[:, :D]) * (HEAD**-0.5)).astype(BF16)
    k = dot(normed, qkv_ref[:, D : 2 * D]).astype(BF16).T
    v = dot(normed, qkv_ref[:, 2 * D :]).astype(BF16)
    low_row = lax.broadcasted_iota(jnp.int32, (1, 128), 1) < HEAD
    even = jnp.where(low_row, 1.0, 0.0).astype(BF16)
    odd = jnp.where(low_row, 0.0, 1.0).astype(BF16)
    low = lax.broadcasted_iota(jnp.int32, (LINE, 128), 1) < HEAD
    wide_low = lax.broadcasted_iota(jnp.int32, (LINE, 256), 1) % 128 < HEAD
    zero = jnp.zeros((128, 128), BF16)

    def diagonal(a, b):
        return jnp.concatenate(
            [jnp.concatenate([a, zero], axis=1), jnp.concatenate([zero, b], axis=1)], axis=0
        )

    exps = [[], []]
    mixed = [[], []]
    for pair in range(n // 2):
        at = 128 * pair
        a, b = slice(at, at + LINE), slice(at + LINE, at + 128)
        cells = []
        for p in range(4):
            c = slice(128 * p, 128 * p + 128)
            top = k[128 * p : 128 * p + 64, at : at + 128]
            bottom = k[128 * p + 64 : 128 * p + 128, at : at + 128]
            cells.append(
                (
                    (
                        q[a, c] * even + q[b, c] * odd,
                        jnp.concatenate([top * even, bottom * odd], axis=0),
                        jnp.concatenate([v[a, c] * even, v[b, c] * odd], axis=0),
                    ),
                    (
                        q[b, c] * even + q[a, c] * odd,
                        jnp.concatenate([top * odd, bottom * even], axis=0),
                        jnp.concatenate([v[a, c] * odd, v[b, c] * even], axis=0),
                    ),
                )
            )
        for g in range(2):
            for i in range(2):
                first, second = cells[2 * g][i], cells[2 * g + 1][i]
                scores = dot(
                    jnp.concatenate([first[0], second[0]], axis=1), diagonal(first[1], second[1])
                )
                e = softmax_top(scores, low)
                exps[i].append(e)
                mixed[i].append(dot(e, diagonal(first[2], second[2])))
    sums = [dot(jnp.concatenate(exps[i], axis=0), ones_block(i)) for i in range(2)]
    rows = []
    for pair in range(n // 2):
        of_a, of_b = [], []
        for g in range(2):
            at = 2 * pair + g
            r = [mixed[i][at] / sums[i][at * LINE : (at + 1) * LINE] for i in range(2)]
            of_a.append(jnp.where(wide_low, r[0], r[1]).astype(BF16))
            of_b.append(jnp.where(wide_low, r[1], r[0]).astype(BF16))
        rows += [jnp.concatenate(of_a, axis=1), jnp.concatenate(of_b, axis=1)]
    return x + dot(jnp.concatenate(rows, axis=0), out_ref[...])


def width_kernel(x_hbm, gain_hbm, qkv_hbm, out_hbm, y_ref, x_ref, gain_ref, qkv_ref, out_ref, sems):
    copies = [
        pltpu.make_async_copy(source, target, sems.at[i])
        for i, (source, target) in enumerate(
            [(x_hbm, x_ref), (gain_hbm, gain_ref), (qkv_hbm.at[0], qkv_ref), (out_hbm.at[0], out_ref)]
        )
    ]
    for copy in copies:
        copy.start()
    for copy in copies:
        copy.wait()
    x = x_ref[...].reshape(TOKENS, D).astype(F32)
    y = attend(x, gain_ref[0:1, :], qkv_ref, out_ref)
    for d in range(2):
        for z in range(8):
            pieces = [y[(d * 8 + h) * LINE + 8 * z :][:8] for h in range(8)]
            y_ref[z, d] = jnp.concatenate(pieces, axis=0).astype(BF16)


def turn(pieces):
    turned = jnp.swapaxes(jnp.concatenate(pieces, axis=0).reshape(8, 8, D), 0, 1)
    return [turned[i] for i in range(8)]


def height_kernel(x_ref, gain_ref, qkv_ref, out_ref, y_ref):
    x = x_ref[...].astype(F32).reshape(2, LINE, 8, D)
    x = jnp.swapaxes(x, 1, 2).reshape(TOKENS, D)
    y = attend(x, gain_ref[1:2, :], qkv_ref, out_ref)
    for wsub in range(2):
        for c in range(2):
            tiles = [
                turn(
                    [
                        y[((zh * 2 + wsub) * 4 + w4) * LINE + (zl * 2 + c) * 8 :][:8]
                        for zh in range(2)
                        for w4 in range(4)
                    ]
                )
                for zl in range(4)
            ]
            for hs in range(8):
                rows = jnp.concatenate([tiles[zl][hs] for zl in range(4)], axis=0)
                y_ref[pl.ds(hs * 128 + wsub * 64 + c * 32, 32), :] = rows.astype(BF16)


def depth_kernel(x_ref, gain_ref, qkv_ref, out_ref, up_ref, down_ref, y_ref):
    x = x_ref[...].astype(F32)
    pieces = {}
    for yh in range(2):
        for d0 in range(2):
            for zl in range(4):
                tile = [x[((yh * 8 + yl) * 2 + d0) * 32 + zl * 8 :][:8] for yl in range(8)]
                for i, piece in enumerate(turn(tile)):
                    pieces[zl, i % 4, i // 4, d0, yh] = piece
    x = jnp.concatenate([pieces[key] for key in sorted(pieces)], axis=0)
    x = attend(x, gain_ref[2:3, :], qkv_ref, out_ref)
    x = x.astype(BF16).astype(F32)
    normed = layer_norm(x, gain_ref[3:4, :])
    total = x
    for part in range(2):
        cols = slice(part * 1024, (part + 1) * 1024)
        hidden = jax.nn.gelu(dot(normed, up_ref[:, cols])).astype(BF16)
        total = total + dot(hidden, down_ref[cols, :])
    pieces = {key: total[8 * i : 8 * i + 8] for i, key in enumerate(sorted(pieces))}
    for zh in range(2):
        for yh in range(2):
            tiles = [
                turn([pieces[zl, w4, zh, d0, yh] for d0 in range(2) for w4 in range(4)])
                for zl in range(4)
            ]
            for yl in range(8):
                rows = jnp.concatenate([tiles[zl][yl] for zl in range(4)], axis=0)
                y_ref[pl.ds((yh * 8 + yl) * 64 + zh * 32, 32), :] = rows.astype(BF16)


def place_kernel(x_ref, y_ref):
    low = lax.broadcasted_iota(jnp.int32, (LINE, D), 0) % 8 < 4
    for hs in range(8):
        first = x_ref[hs, 0].astype(F32)
        second = x_ref[hs, 1].astype(F32)
        y_ref[0, hs] = jnp.where(low, first, pltpu.roll(second, 4, 0)).astype(BF16)
        y_ref[1, hs] = jnp.where(low, pltpu.roll(first, LINE - 4, 0), second).astype(BF16)


PARAMS = pltpu.CompilerParams(vmem_limit_bytes=40 * 1024 * 1024)


def weight_specs(layer):
    return [
        pl.BlockSpec((4, D), lambda *i: (0, 0)),
        pl.BlockSpec((None, D, 3 * D), lambda *i: (layer, 0, 0)),
        pl.BlockSpec((None, D, D), lambda *i: (layer, 0, 0)),
    ]


def whole(*shape):
    return pl.BlockSpec(shape, lambda *i: (0,) * len(shape))


def body(volume, qkv_weight, out_weight, norm_gain, up_weight, down_weight):
    weights = (norm_gain, qkv_weight, out_weight)
    sent = pl.pallas_call(
        width_kernel,
        in_specs=[pl.BlockSpec(memory_space=pltpu.HBM)] * 4,
        out_specs=pl.BlockSpec(memory_space=pltpu.VMEM),
        out_shape=jax.ShapeDtypeStruct((8, 2, 64, D), BF16),
        scratch_shapes=[
            pltpu.VMEM((2, 8, LINE, D), BF16),
            pltpu.VMEM((4, D), F32),
            pltpu.VMEM((D, 3 * D), BF16),
            pltpu.VMEM((D, D), BF16),
            pltpu.SemaphoreType.DMA((4,)),
        ],
        compiler_params=PARAMS,
        name="width",
    )(*[pltpu.with_memory_space_constraint(a, pltpu.HBM) for a in (volume, *weights)])
    sent = sent.reshape(16, 64, D)
    held = lax.all_to_all(sent, ("zh", "zl", "c"), split_axis=0, concat_axis=0, tiled=True)
    sent = pl.pallas_call(
        height_kernel,
        grid=(1,),
        in_specs=[whole(TOKENS, D)] + weight_specs(1),
        out_specs=whole(TOKENS, D),
        out_shape=jax.ShapeDtypeStruct((TOKENS, D), BF16),
        compiler_params=PARAMS,
        name="height",
    )(held.reshape(TOKENS, D), *weights)
    sent = sent.reshape(32, 32, D)
    held = lax.all_to_all(sent, ("y", "x", "c"), split_axis=0, concat_axis=0, tiled=True)
    sent = pl.pallas_call(
        depth_kernel,
        grid=(1,),
        in_specs=[whole(TOKENS, D)] + weight_specs(2) + [whole(D, FF), whole(FF, D)],
        out_specs=whole(TOKENS, D),
        out_shape=jax.ShapeDtypeStruct((TOKENS, D), BF16),
        compiler_params=PARAMS,
        name="depth",
    )(held.reshape(TOKENS, D), *weights, up_weight, down_weight)
    sent = sent.reshape(128, 8, D)
    held = lax.all_to_all(sent, ("y", "x", "zh", "zl"), split_axis=0, concat_axis=0, tiled=True)
    return pl.pallas_call(
        place_kernel,
        grid=(1,),
        in_specs=[whole(8, 2, LINE, D)],
        out_specs=whole(2, 8, LINE, D),
        out_shape=jax.ShapeDtypeStruct((2, 8, LINE, D), BF16),
        compiler_params=PARAMS,
        name="place",
    )(held.reshape(8, 2, LINE, D))


def solution(mesh):
    fine = Mesh(mesh.devices.reshape(4, 4, 2, 4, 2), ("y", "x", "zh", "zl", "c"))
    return jax.shard_map(
        body,
        mesh=fine,
        in_specs=(P(("y", "x", "zh"), ("zl", "c"), None, None), P(), P(), P(), P(), P()),
        out_specs=P(("y", "x", "zh"), ("zl", "c"), None, None),
        check_vma=False,
    )
```

```python
import jax
import jax.numpy as jnp
from jax import lax
from jax.experimental import pallas as pl
from jax.experimental.pallas import tpu as pltpu
from jax.sharding import Mesh
from jax.sharding import PartitionSpec as P

D = 512
HEADS = 8
HEAD = 64
FF = 2048
LINE = 64
TOKENS = 1024
EPS = 1e-5
F32 = jnp.float32
BF16 = jnp.bfloat16


def layer_norm(x, gain):
    center = jnp.mean(x, axis=-1, keepdims=True)
    shifted = x - center
    spread = jnp.mean(shifted * shifted, axis=-1, keepdims=True)
    return (shifted * lax.rsqrt(spread + EPS) * gain).astype(BF16)


def dot(a, b):
    return jnp.dot(a, b, preferred_element_type=F32)


def softmax_top(scores, low):
    parts = []
    for half in range(2):
        s = scores[:, half * 128 : (half + 1) * 128]
        top_low = jnp.max(jnp.where(low, s, -jnp.inf), axis=-1, keepdims=True)
        top_high = jnp.max(jnp.where(low, -jnp.inf, s), axis=-1, keepdims=True)
        parts.append(jnp.exp(s - jnp.where(low, top_low, top_high)).astype(BF16))
    return jnp.concatenate(parts, axis=1)


def ones_block(crossed):
    row = lax.broadcasted_iota(jnp.int32, (256, 256), 0) // HEAD
    column = lax.broadcasted_iota(jnp.int32, (256, 256), 1) // HEAD
    if crossed:
        column = column + 1 - 2 * (column % 2)
    return jnp.where(row == column, 1.0, 0.0).astype(BF16)


def attend(x, gain, qkv_ref, out_ref):
    n = x.shape[0] // LINE
    normed = layer_norm(x, gain)
    q = (dot(normed, qkv_ref[:, :D]) * (HEAD**-0.5)).astype(BF16)
    k = dot(normed, qkv_ref[:, D : 2 * D]).astype(BF16).T
    v = dot(normed, qkv_ref[:, 2 * D :]).astype(BF16)
    low_row = lax.broadcasted_iota(jnp.int32, (1, 128), 1) < HEAD
    even = jnp.where(low_row, 1.0, 0.0).astype(BF16)
    odd = jnp.where(low_row, 0.0, 1.0).astype(BF16)
    low = lax.broadcasted_iota(jnp.int32, (LINE, 128), 1) < HEAD
    wide_low = lax.broadcasted_iota(jnp.int32, (LINE, 256), 1) % 128 < HEAD
    zero = jnp.zeros((128, 128), BF16)

    def diagonal(a, b):
        return jnp.concatenate(
            [jnp.concatenate([a, zero], axis=1), jnp.concatenate([zero, b], axis=1)], axis=0
        )

    exps = [[], []]
    mixed = [[], []]
    for pair in range(n // 2):
        at = 128 * pair
        a, b = slice(at, at + LINE), slice(at + LINE, at + 128)
        cells = []
        for p in range(4):
            c = slice(128 * p, 128 * p + 128)
            top = k[128 * p : 128 * p + 64, at : at + 128]
            bottom = k[128 * p + 64 : 128 * p + 128, at : at + 128]
            cells.append(
                (
                    (
                        q[a, c] * even + q[b, c] * odd,
                        jnp.concatenate([top * even, bottom * odd], axis=0),
                        jnp.concatenate([v[a, c] * even, v[b, c] * odd], axis=0),
                    ),
                    (
                        q[b, c] * even + q[a, c] * odd,
                        jnp.concatenate([top * odd, bottom * even], axis=0),
                        jnp.concatenate([v[a, c] * odd, v[b, c] * even], axis=0),
                    ),
                )
            )
        for g in range(2):
            for i in range(2):
                first, second = cells[2 * g][i], cells[2 * g + 1][i]
                scores = dot(
                    jnp.concatenate([first[0], second[0]], axis=1), diagonal(first[1], second[1])
                )
                e = softmax_top(scores, low)
                exps[i].append(e)
                mixed[i].append(dot(e, diagonal(first[2], second[2])))
    sums = [dot(jnp.concatenate(exps[i], axis=0), ones_block(i)) for i in range(2)]
    rows = []
    for pair in range(n // 2):
        of_a, of_b = [], []
        for g in range(2):
            at = 2 * pair + g
            r = [mixed[i][at] / sums[i][at * LINE : (at + 1) * LINE] for i in range(2)]
            of_a.append(jnp.where(wide_low, r[0], r[1]).astype(BF16))
            of_b.append(jnp.where(wide_low, r[1], r[0]).astype(BF16))
        rows += [jnp.concatenate(of_a, axis=1), jnp.concatenate(of_b, axis=1)]
    return x + dot(jnp.concatenate(rows, axis=0), out_ref[...])


def width_kernel(x_hbm, gain_hbm, qkv_hbm, out_hbm, y_ref, x_ref, gain_ref, qkv_ref, out_ref, sems):
    copies = [
        pltpu.make_async_copy(source, target, sems.at[i])
        for i, (source, target) in enumerate(
            [(x_hbm, x_ref), (gain_hbm, gain_ref), (qkv_hbm.at[0], qkv_ref), (out_hbm.at[0], out_ref)]
        )
    ]
    for copy in copies:
        copy.start()
    for copy in copies:
        copy.wait()
    x = x_ref[...].reshape(TOKENS, D).astype(F32)
    y = attend(x, gain_ref[0:1, :], qkv_ref, out_ref)
    for d in range(2):
        for z in range(8):
            pieces = [y[(d * 8 + h) * LINE + 8 * z :][:8] for h in range(8)]
            y_ref[z, d] = jnp.concatenate(pieces, axis=0).astype(BF16)


def turn(pieces):
    turned = jnp.swapaxes(jnp.concatenate(pieces, axis=0).reshape(8, 8, D), 0, 1)
    return [turned[i] for i in range(8)]


def height_kernel(x_ref, gain_ref, qkv_ref, out_ref, y_ref):
    x = x_ref[...].astype(F32).reshape(2, LINE, 8, D)
    x = jnp.swapaxes(x, 1, 2).reshape(TOKENS, D)
    y = attend(x, gain_ref[1:2, :], qkv_ref, out_ref)
    for wsub in range(2):
        for c in range(2):
            tiles = [
                turn(
                    [
                        y[((zh * 2 + wsub) * 4 + w4) * LINE + (zl * 2 + c) * 8 :][:8]
                        for zh in range(2)
                        for w4 in range(4)
                    ]
                )
                for zl in range(4)
            ]
            for hs in range(8):
                rows = jnp.concatenate([tiles[zl][hs] for zl in range(4)], axis=0)
                y_ref[pl.ds(hs * 128 + wsub * 64 + c * 32, 32), :] = rows.astype(BF16)


def depth_kernel(x_ref, gain_ref, qkv_ref, out_ref, up_ref, down_ref, y_ref):
    x = x_ref[...].astype(F32)
    pieces = {}
    for yh in range(2):
        for d0 in range(2):
            for zl in range(4):
                tile = [x[((yh * 8 + yl) * 2 + d0) * 32 + zl * 8 :][:8] for yl in range(8)]
                for i, piece in enumerate(turn(tile)):
                    pieces[zl, i % 4, i // 4, d0, yh] = piece
    x = jnp.concatenate([pieces[key] for key in sorted(pieces)], axis=0)
    x = attend(x, gain_ref[2:3, :], qkv_ref, out_ref)
    x = x.astype(BF16).astype(F32)
    normed = layer_norm(x, gain_ref[3:4, :])
    total = x
    for part in range(2):
        cols = slice(part * 1024, (part + 1) * 1024)
        hidden = jax.nn.gelu(dot(normed, up_ref[:, cols])).astype(BF16)
        total = total + dot(hidden, down_ref[cols, :])
    pieces = {key: total[8 * i : 8 * i + 8] for i, key in enumerate(sorted(pieces))}
    for zh in range(2):
        for yh in range(2):
            tiles = [
                turn([pieces[zl, w4, zh, d0, yh] for d0 in range(2) for w4 in range(4)])
                for zl in range(4)
            ]
            for y in range(2):
                for zl in range(4):
                    rows = jnp.concatenate(tiles[zl][4 * y : 4 * y + 4], axis=0)
                    at = ((yh * 2 + y) * 8 + zh * 4 + zl) * 32
                    y_ref[pl.ds(at, 32), :] = rows.astype(BF16)


def place_kernel(x_ref, y_ref):
    low = lax.broadcasted_iota(jnp.int32, (LINE, D), 0) % 8 < 4
    for hs in range(8):
        first = x_ref[hs // 2, :, hs % 2 * 2].reshape(LINE, D).astype(F32)
        second = x_ref[hs // 2, :, hs % 2 * 2 + 1].reshape(LINE, D).astype(F32)
        y_ref[0, hs] = jnp.where(low, first, pltpu.roll(second, 4, 0)).astype(BF16)
        y_ref[1, hs] = jnp.where(low, pltpu.roll(first, LINE - 4, 0), second).astype(BF16)


PARAMS = pltpu.CompilerParams(vmem_limit_bytes=40 * 1024 * 1024)


def weight_specs(layer):
    return [
        pl.BlockSpec((4, D), lambda *i: (0, 0)),
        pl.BlockSpec((None, D, 3 * D), lambda *i: (layer, 0, 0)),
        pl.BlockSpec((None, D, D), lambda *i: (layer, 0, 0)),
    ]


def whole(*shape):
    return pl.BlockSpec(shape, lambda *i: (0,) * len(shape))


def body(volume, qkv_weight, out_weight, norm_gain, up_weight, down_weight):
    weights = (norm_gain, qkv_weight, out_weight)
    sent = pl.pallas_call(
        width_kernel,
        in_specs=[pl.BlockSpec(memory_space=pltpu.HBM)] * 4,
        out_specs=pl.BlockSpec(memory_space=pltpu.VMEM),
        out_shape=jax.ShapeDtypeStruct((8, 2, 64, D), BF16),
        scratch_shapes=[
            pltpu.VMEM((2, 8, LINE, D), BF16),
            pltpu.VMEM((4, D), F32),
            pltpu.VMEM((D, 3 * D), BF16),
            pltpu.VMEM((D, D), BF16),
            pltpu.SemaphoreType.DMA((4,)),
        ],
        compiler_params=PARAMS,
        name="width",
    )(*[pltpu.with_memory_space_constraint(a, pltpu.HBM) for a in (volume, *weights)])
    sent = sent.reshape(16, 64, D)
    held = lax.all_to_all(sent, ("zh", "zl", "c"), split_axis=0, concat_axis=0, tiled=True)
    sent = pl.pallas_call(
        height_kernel,
        grid=(1,),
        in_specs=[whole(TOKENS, D)] + weight_specs(1),
        out_specs=whole(TOKENS, D),
        out_shape=jax.ShapeDtypeStruct((TOKENS, D), BF16),
        compiler_params=PARAMS,
        name="height",
    )(held.reshape(TOKENS, D), *weights)
    sent = sent.reshape(32, 32, D)
    held = lax.all_to_all(sent, ("y", "x", "c"), split_axis=0, concat_axis=0, tiled=True)
    sent = pl.pallas_call(
        depth_kernel,
        grid=(1,),
        in_specs=[whole(TOKENS, D)] + weight_specs(2) + [whole(D, FF), whole(FF, D)],
        out_specs=whole(TOKENS, D),
        out_shape=jax.ShapeDtypeStruct((TOKENS, D), BF16),
        compiler_params=PARAMS,
        name="depth",
    )(held.reshape(TOKENS, D), *weights, up_weight, down_weight)
    sent = sent.reshape(128, 8, D)
    held = lax.all_to_all(sent, ("y", "zh", "zl", "x"), split_axis=0, concat_axis=0, tiled=True)
    return pl.pallas_call(
        place_kernel,
        grid=(1,),
        in_specs=[whole(4, 8, 4, 8, D)],
        out_specs=whole(2, 8, LINE, D),
        out_shape=jax.ShapeDtypeStruct((2, 8, LINE, D), BF16),
        compiler_params=PARAMS,
        name="place",
    )(held.reshape(4, 8, 4, 8, D))


def solution(mesh):
    fine = Mesh(mesh.devices.reshape(4, 4, 2, 4, 2), ("y", "x", "zh", "zl", "c"))
    return jax.shard_map(
        body,
        mesh=fine,
        in_specs=(P(("y", "x", "zh"), ("zl", "c"), None, None), P(), P(), P(), P(), P()),
        out_specs=P(("y", "x", "zh"), ("zl", "c"), None, None),
        check_vma=False,
    )
```

```python
import jax
import jax.numpy as jnp
from jax import lax
from jax.experimental import pallas as pl
from jax.experimental.pallas import tpu as pltpu
from jax.sharding import Mesh
from jax.sharding import PartitionSpec as P

D = 512
HEADS = 8
HEAD = 64
FF = 2048
LINE = 64
TOKENS = 1024
EPS = 1e-5
F32 = jnp.float32
BF16 = jnp.bfloat16


def layer_norm(x, gain):
    center = jnp.mean(x, axis=-1, keepdims=True)
    shifted = x - center
    spread = jnp.mean(shifted * shifted, axis=-1, keepdims=True)
    return (shifted * lax.rsqrt(spread + EPS) * gain).astype(BF16)


def dot(a, b):
    return jnp.dot(a, b, preferred_element_type=F32)


def softmax_top(scores, low):
    parts = []
    for half in range(2):
        s = scores[:, half * 128 : (half + 1) * 128]
        top_low = jnp.max(jnp.where(low, s, -jnp.inf), axis=-1, keepdims=True)
        top_high = jnp.max(jnp.where(low, -jnp.inf, s), axis=-1, keepdims=True)
        parts.append(jnp.exp(s - jnp.where(low, top_low, top_high)).astype(BF16))
    return jnp.concatenate(parts, axis=1)


def ones_block(crossed):
    row = lax.broadcasted_iota(jnp.int32, (256, 256), 0) // HEAD
    column = lax.broadcasted_iota(jnp.int32, (256, 256), 1) // HEAD
    if crossed:
        column = column + 1 - 2 * (column % 2)
    return jnp.where(row == column, 1.0, 0.0).astype(BF16)


def attend(x, gain, qkv_ref, out_ref):
    n = x.shape[0] // LINE
    normed = layer_norm(x, gain)
    q = (dot(normed, qkv_ref[:, :D]) * (HEAD**-0.5)).astype(BF16)
    k = dot(normed, qkv_ref[:, D : 2 * D]).astype(BF16).T
    v = dot(normed, qkv_ref[:, 2 * D :]).astype(BF16)
    low_row = lax.broadcasted_iota(jnp.int32, (1, 128), 1) < HEAD
    even = jnp.where(low_row, 1.0, 0.0).astype(BF16)
    odd = jnp.where(low_row, 0.0, 1.0).astype(BF16)
    low = lax.broadcasted_iota(jnp.int32, (LINE, 128), 1) < HEAD
    wide_low = lax.broadcasted_iota(jnp.int32, (LINE, 256), 1) % 128 < HEAD
    zero = jnp.zeros((128, 128), BF16)

    def diagonal(a, b):
        return jnp.concatenate(
            [jnp.concatenate([a, zero], axis=1), jnp.concatenate([zero, b], axis=1)], axis=0
        )

    exps = [[], []]
    mixed = [[], []]
    for pair in range(n // 2):
        at = 128 * pair
        a, b = slice(at, at + LINE), slice(at + LINE, at + 128)
        cells = []
        for p in range(4):
            c = slice(128 * p, 128 * p + 128)
            top = k[128 * p : 128 * p + 64, at : at + 128]
            bottom = k[128 * p + 64 : 128 * p + 128, at : at + 128]
            cells.append(
                (
                    (
                        q[a, c] * even + q[b, c] * odd,
                        jnp.concatenate([top * even, bottom * odd], axis=0),
                        jnp.concatenate([v[a, c] * even, v[b, c] * odd], axis=0),
                    ),
                    (
                        q[b, c] * even + q[a, c] * odd,
                        jnp.concatenate([top * odd, bottom * even], axis=0),
                        jnp.concatenate([v[a, c] * odd, v[b, c] * even], axis=0),
                    ),
                )
            )
        for g in range(2):
            for i in range(2):
                first, second = cells[2 * g][i], cells[2 * g + 1][i]
                scores = dot(
                    jnp.concatenate([first[0], second[0]], axis=1), diagonal(first[1], second[1])
                )
                e = softmax_top(scores, low)
                exps[i].append(e)
                mixed[i].append(dot(e, diagonal(first[2], second[2])))
    sums = [dot(jnp.concatenate(exps[i], axis=0), ones_block(i)) for i in range(2)]
    rows = []
    for pair in range(n // 2):
        of_a, of_b = [], []
        for g in range(2):
            at = 2 * pair + g
            r = [mixed[i][at] / sums[i][at * LINE : (at + 1) * LINE] for i in range(2)]
            of_a.append(jnp.where(wide_low, r[0], r[1]).astype(BF16))
            of_b.append(jnp.where(wide_low, r[1], r[0]).astype(BF16))
        rows += [jnp.concatenate(of_a, axis=1), jnp.concatenate(of_b, axis=1)]
    return x + dot(jnp.concatenate(rows, axis=0), out_ref[...])


def own_z():
    return lax.axis_index("zh") * 4 + lax.axis_index("zl")


def by_distance(y, y_ref):
    here = own_z()
    for z in range(8):
        pieces = [y[h * LINE + 8 * z :][:8] for h in range(8)]
        y_ref[lax.rem(z + 8 - here, 8)] = jnp.concatenate(pieces, axis=0).astype(BF16)


def width_away_kernel(
    x_hbm, gain_hbm, qkv_hbm, out_hbm, y_ref, home_ref, gain_ref, qkv_ref, out_ref, x_ref, sems
):
    core = lax.axis_index("c")
    copies = [
        pltpu.make_async_copy(source, target, sems.at[i])
        for i, (source, target) in enumerate(
            [
                (x_hbm.at[1 - core], x_ref),
                (gain_hbm, gain_ref),
                (qkv_hbm.at[0], qkv_ref),
                (out_hbm.at[0], out_ref),
                (x_hbm.at[core], home_ref),
            ]
        )
    ]
    for copy in copies:
        copy.start()
    for copy in copies[:4]:
        copy.wait()
    x = x_ref[...].reshape(8 * LINE, D).astype(F32)
    by_distance(attend(x, gain_ref[0:1, :], qkv_ref, out_ref), y_ref)
    copies[4].wait()


def width_home_kernel(x_ref, gain_ref, qkv_ref, out_ref, y_ref):
    x = x_ref[...].reshape(8 * LINE, D).astype(F32)
    by_distance(attend(x, gain_ref[0:1, :], qkv_ref, out_ref), y_ref)


def turn(pieces):
    turned = jnp.swapaxes(jnp.concatenate(pieces, axis=0).reshape(8, 8, D), 0, 1)
    return [turned[i] for i in range(8)]


def height_kernel(*refs):
    *blocks, gain_ref, qkv_ref, out_ref, y_ref, x_ref = refs
    here, own_core = own_z(), lax.axis_index("c")
    for distance, block in zip(DISTANCES, blocks):
        for core in range(2):
            x_ref[lax.rem(here + 8 - distance, 8), lax.bitwise_xor(own_core, core)] = block[core]
    x = x_ref[...].astype(F32).reshape(2, LINE, 8, D)
    x = jnp.swapaxes(x, 1, 2).reshape(TOKENS, D)
    y = attend(x, gain_ref[1:2, :], qkv_ref, out_ref)
    for wsub in range(2):
        for c in range(2):
            tiles = [
                turn(
                    [
                        y[((zh * 2 + wsub) * 4 + w4) * LINE + (zl * 2 + c) * 8 :][:8]
                        for zh in range(2)
                        for w4 in range(4)
                    ]
                )
                for zl in range(4)
            ]
            for hs in range(8):
                rows = jnp.concatenate([tiles[zl][hs] for zl in range(4)], axis=0)
                y_ref[pl.ds(hs * 128 + wsub * 64 + c * 32, 32), :] = rows.astype(BF16)


def depth_kernel(x_ref, gain_ref, qkv_ref, out_ref, up_ref, down_ref, y_ref):
    x = x_ref[...].astype(F32)
    pieces = {}
    for yh in range(2):
        for d0 in range(2):
            for zl in range(4):
                tile = [x[((yh * 8 + yl) * 2 + d0) * 32 + zl * 8 :][:8] for yl in range(8)]
                for i, piece in enumerate(turn(tile)):
                    pieces[zl, i % 4, i // 4, d0, yh] = piece
    x = jnp.concatenate([pieces[key] for key in sorted(pieces)], axis=0)
    x = attend(x, gain_ref[2:3, :], qkv_ref, out_ref)
    x = x.astype(BF16).astype(F32)
    normed = layer_norm(x, gain_ref[3:4, :])
    total = x
    for part in range(2):
        cols = slice(part * 1024, (part + 1) * 1024)
        hidden = jax.nn.gelu(dot(normed, up_ref[:, cols])).astype(BF16)
        total = total + dot(hidden, down_ref[cols, :])
    pieces = {key: total[8 * i : 8 * i + 8] for i, key in enumerate(sorted(pieces))}
    for zh in range(2):
        for yh in range(2):
            tiles = [
                turn([pieces[zl, w4, zh, d0, yh] for d0 in range(2) for w4 in range(4)])
                for zl in range(4)
            ]
            for y in range(2):
                for zl in range(4):
                    rows = jnp.concatenate(tiles[zl][4 * y : 4 * y + 4], axis=0)
                    at = ((yh * 2 + y) * 8 + zh * 4 + zl) * 32
                    y_ref[pl.ds(at, 32), :] = rows.astype(BF16)


def place_kernel(x_ref, y_ref):
    low = lax.broadcasted_iota(jnp.int32, (LINE, D), 0) % 8 < 4
    for hs in range(8):
        first = x_ref[hs // 2, :, hs % 2 * 2].reshape(LINE, D).astype(F32)
        second = x_ref[hs // 2, :, hs % 2 * 2 + 1].reshape(LINE, D).astype(F32)
        y_ref[0, hs] = jnp.where(low, first, pltpu.roll(second, 4, 0)).astype(BF16)
        y_ref[1, hs] = jnp.where(low, pltpu.roll(first, LINE - 4, 0), second).astype(BF16)


PARAMS = pltpu.CompilerParams(vmem_limit_bytes=40 * 1024 * 1024)
DISTANCES = (0, 1, 7, 3, 5, 4, 2, 6)
IN_HBM = pl.BlockSpec(memory_space=pltpu.HBM)
IN_VMEM = pl.BlockSpec(memory_space=pltpu.VMEM)


def weight_specs(layer):
    return [
        pl.BlockSpec((4, D), lambda *i: (0, 0)),
        pl.BlockSpec((None, D, 3 * D), lambda *i: (layer, 0, 0)),
        pl.BlockSpec((None, D, D), lambda *i: (layer, 0, 0)),
    ]


def whole(*shape):
    return pl.BlockSpec(shape, lambda *i: (0,) * len(shape))


def cost(nanoseconds):
    return pl.CostEstimate(flops=700_000 * nanoseconds, bytes_accessed=1 << 20, transcendentals=0)


def phase(kernel, shape, *operands, **options):
    return pl.pallas_call(
        kernel,
        in_specs=[IN_VMEM] * len(operands),
        out_specs=IN_VMEM,
        out_shape=jax.ShapeDtypeStruct(shape, BF16),
        compiler_params=PARAMS,
        **options,
    )(*operands)


def body(volume, qkv_weight, out_weight, norm_gain, up_weight, down_weight):
    weights = (norm_gain, qkv_weight, out_weight)
    half = (8, LINE, D)
    away, home, *first_weights = pl.pallas_call(
        width_away_kernel,
        in_specs=[IN_HBM] * 4,
        out_specs=[IN_VMEM] * 5,
        out_shape=[
            jax.ShapeDtypeStruct(half, BF16),
            jax.ShapeDtypeStruct(half, BF16),
            jax.ShapeDtypeStruct((4, D), F32),
            jax.ShapeDtypeStruct((D, 3 * D), BF16),
            jax.ShapeDtypeStruct((D, D), BF16),
        ],
        scratch_shapes=[pltpu.VMEM(half, BF16), pltpu.SemaphoreType.DMA((5,))],
        compiler_params=PARAMS,
        name="width_away",
    )(*[pltpu.with_memory_space_constraint(a, pltpu.HBM) for a in (volume, *weights)])
    away = lax.ppermute(away, "c", [(0, 1), (1, 0)])
    home = phase(width_home_kernel, half, home, *first_weights, name="width_home", cost_estimate=cost(3000))
    blocks = [jnp.stack([home[i], away[i]]) for i in range(8)]
    held = blocks[:1] + [
        lax.ppermute(blocks[i], ("zh", "zl"), [(z, (z + i) % 8) for z in range(8)]) for i in DISTANCES[1:]
    ]
    sent = pl.pallas_call(
        height_kernel,
        grid=(1,),
        in_specs=[whole(2, LINE, D)] * 8 + weight_specs(1),
        out_specs=whole(TOKENS, D),
        out_shape=jax.ShapeDtypeStruct((TOKENS, D), BF16),
        scratch_shapes=[pltpu.VMEM((8, 2, LINE, D), BF16)],
        compiler_params=PARAMS,
        name="height",
    )(*held, *weights)
    sent = sent.reshape(32, 32, D)
    held = lax.all_to_all(sent, ("y", "x", "c"), split_axis=0, concat_axis=0, tiled=True)
    sent = pl.pallas_call(
        depth_kernel,
        grid=(1,),
        in_specs=[whole(TOKENS, D)] + weight_specs(2) + [whole(D, FF), whole(FF, D)],
        out_specs=whole(TOKENS, D),
        out_shape=jax.ShapeDtypeStruct((TOKENS, D), BF16),
        compiler_params=PARAMS,
        name="depth",
    )(held.reshape(TOKENS, D), *weights, up_weight, down_weight)
    sent = sent.reshape(128, 8, D)
    held = lax.all_to_all(sent, ("y", "zh", "zl", "x"), split_axis=0, concat_axis=0, tiled=True)
    return pl.pallas_call(
        place_kernel,
        grid=(1,),
        in_specs=[whole(4, 8, 4, 8, D)],
        out_specs=whole(2, 8, LINE, D),
        out_shape=jax.ShapeDtypeStruct((2, 8, LINE, D), BF16),
        compiler_params=PARAMS,
        name="place",
    )(held.reshape(4, 8, 4, 8, D))


def solution(mesh):
    fine = Mesh(mesh.devices.reshape(4, 4, 2, 4, 2), ("y", "x", "zh", "zl", "c"))
    return jax.shard_map(
        body,
        mesh=fine,
        in_specs=(P(("y", "x", "zh"), ("zl", "c"), None, None), P(), P(), P(), P(), P()),
        out_specs=P(("y", "x", "zh"), ("zl", "c"), None, None),
        check_vma=False,
    )
```

```python
import jax
import jax.numpy as jnp
from jax import lax
from jax.experimental import pallas as pl
from jax.experimental.pallas import tpu as pltpu
from jax.sharding import Mesh
from jax.sharding import PartitionSpec as P

D = 512
HEADS = 8
HEAD = 64
FF = 2048
LINE = 64
TOKENS = 1024
EPS = 1e-5
F32 = jnp.float32
BF16 = jnp.bfloat16


def layer_norm(x, gain):
    center = jnp.mean(x, axis=-1, keepdims=True)
    shifted = x - center
    spread = jnp.mean(shifted * shifted, axis=-1, keepdims=True)
    return (shifted * lax.rsqrt(spread + EPS) * gain).astype(BF16)


def dot(a, b):
    return jnp.dot(a, b, preferred_element_type=F32)


def softmax_top(scores, low):
    parts = []
    for half in range(2):
        s = scores[:, half * 128 : (half + 1) * 128]
        top_low = jnp.max(jnp.where(low, s, -jnp.inf), axis=-1, keepdims=True)
        top_high = jnp.max(jnp.where(low, -jnp.inf, s), axis=-1, keepdims=True)
        parts.append(jnp.exp(s - jnp.where(low, top_low, top_high)).astype(BF16))
    return jnp.concatenate(parts, axis=1)


def ones_block(crossed):
    row = lax.broadcasted_iota(jnp.int32, (256, 256), 0) // HEAD
    column = lax.broadcasted_iota(jnp.int32, (256, 256), 1) // HEAD
    if crossed:
        column = column + 1 - 2 * (column % 2)
    return jnp.where(row == column, 1.0, 0.0).astype(BF16)


def attend(x, gain, qkv_ref, out_ref, ready=None):
    n = x.shape[0] // LINE
    normed = layer_norm(x, gain)
    if ready:
        ready()
    q = (dot(normed, qkv_ref[:, :D]) * (HEAD**-0.5)).astype(BF16)
    k = dot(normed, qkv_ref[:, D : 2 * D]).astype(BF16).T
    v = dot(normed, qkv_ref[:, 2 * D :]).astype(BF16)
    low_row = lax.broadcasted_iota(jnp.int32, (1, 128), 1) < HEAD
    even = jnp.where(low_row, 1.0, 0.0).astype(BF16)
    odd = jnp.where(low_row, 0.0, 1.0).astype(BF16)
    low = lax.broadcasted_iota(jnp.int32, (LINE, 128), 1) < HEAD
    wide_low = lax.broadcasted_iota(jnp.int32, (LINE, 256), 1) % 128 < HEAD
    zero = jnp.zeros((128, 128), BF16)

    def diagonal(a, b):
        return jnp.concatenate(
            [jnp.concatenate([a, zero], axis=1), jnp.concatenate([zero, b], axis=1)], axis=0
        )

    exps = [[], []]
    mixed = [[], []]
    for pair in range(n // 2):
        at = 128 * pair
        a, b = slice(at, at + LINE), slice(at + LINE, at + 128)
        cells = []
        for p in range(4):
            c = slice(128 * p, 128 * p + 128)
            top = k[128 * p : 128 * p + 64, at : at + 128]
            bottom = k[128 * p + 64 : 128 * p + 128, at : at + 128]
            cells.append(
                (
                    (
                        q[a, c] * even + q[b, c] * odd,
                        jnp.concatenate([top * even, bottom * odd], axis=0),
                        jnp.concatenate([v[a, c] * even, v[b, c] * odd], axis=0),
                    ),
                    (
                        q[b, c] * even + q[a, c] * odd,
                        jnp.concatenate([top * odd, bottom * even], axis=0),
                        jnp.concatenate([v[a, c] * odd, v[b, c] * even], axis=0),
                    ),
                )
            )
        for g in range(2):
            for i in range(2):
                first, second = cells[2 * g][i], cells[2 * g + 1][i]
                scores = dot(
                    jnp.concatenate([first[0], second[0]], axis=1), diagonal(first[1], second[1])
                )
                e = softmax_top(scores, low)
                exps[i].append(e)
                mixed[i].append(dot(e, diagonal(first[2], second[2])))
    sums = [dot(jnp.concatenate(exps[i], axis=0), ones_block(i)) for i in range(2)]
    rows = []
    for pair in range(n // 2):
        of_a, of_b = [], []
        for g in range(2):
            at = 2 * pair + g
            r = [mixed[i][at] / sums[i][at * LINE : (at + 1) * LINE] for i in range(2)]
            of_a.append(jnp.where(wide_low, r[0], r[1]).astype(BF16))
            of_b.append(jnp.where(wide_low, r[1], r[0]).astype(BF16))
        rows += [jnp.concatenate(of_a, axis=1), jnp.concatenate(of_b, axis=1)]
    return x + dot(jnp.concatenate(rows, axis=0), out_ref[...])


def own_z():
    return lax.axis_index("zh") * 4 + lax.axis_index("zl")


def by_distance(y, y_ref):
    here = own_z()
    for z in range(8):
        pieces = [y[h * LINE + 8 * z :][:8] for h in range(8)]
        y_ref[lax.rem(z + 8 - here, 8)] = jnp.concatenate(pieces, axis=0).astype(BF16)


def width_away_kernel(
    x_hbm, gain_hbm, qkv_hbm, out_hbm, y_ref, home_ref, gain_ref, qkv_ref, out_ref, x_ref, sems
):
    core = lax.axis_index("c")
    copies = [
        pltpu.make_async_copy(source, target, sems.at[i])
        for i, (source, target) in enumerate(
            [
                (x_hbm.at[1 - core], x_ref),
                (gain_hbm, gain_ref),
                (qkv_hbm.at[0], qkv_ref),
                (out_hbm.at[0], out_ref),
                (x_hbm.at[core], home_ref),
            ]
        )
    ]
    for copy in copies:
        copy.start()
    def ready():
        for copy in copies[2:4]:
            copy.wait()

    for copy in copies[:2]:
        copy.wait()
    x = x_ref[...].reshape(8 * LINE, D).astype(F32)
    by_distance(attend(x, gain_ref[0:1, :], qkv_ref, out_ref, ready), y_ref)
    copies[4].wait()


def width_home_kernel(x_ref, gain_ref, qkv_ref, out_ref, y_ref):
    x = x_ref[...].reshape(8 * LINE, D).astype(F32)
    by_distance(attend(x, gain_ref[0:1, :], qkv_ref, out_ref), y_ref)


def turn(pieces):
    turned = jnp.swapaxes(jnp.concatenate(pieces, axis=0).reshape(8, 8, D), 0, 1)
    return [turned[i] for i in range(8)]


def height_kernel(*refs):
    *blocks, gain_ref, qkv_ref, out_ref, y_ref, x_ref = refs
    here, own_core = own_z(), lax.axis_index("c")
    for distance, block in zip(DISTANCES, blocks):
        for core in range(2):
            x_ref[lax.rem(here + 8 - distance, 8), lax.bitwise_xor(own_core, core)] = block[core]
    x = x_ref[...].astype(F32).reshape(2, LINE, 8, D)
    x = jnp.swapaxes(x, 1, 2).reshape(TOKENS, D)
    y = attend(x, gain_ref[1:2, :], qkv_ref, out_ref)
    for wsub in range(2):
        for c in range(2):
            tiles = [
                turn(
                    [
                        y[((zh * 2 + wsub) * 4 + w4) * LINE + (zl * 2 + c) * 8 :][:8]
                        for zh in range(2)
                        for w4 in range(4)
                    ]
                )
                for zl in range(4)
            ]
            for hs in range(8):
                rows = jnp.concatenate([tiles[zl][hs] for zl in range(4)], axis=0)
                y_ref[pl.ds(hs * 128 + wsub * 64 + c * 32, 32), :] = rows.astype(BF16)


def depth_kernel(x_ref, gain_ref, qkv_ref, out_ref, up_ref, down_ref, y_ref):
    x = x_ref[...].astype(F32)
    pieces = {}
    for yh in range(2):
        for d0 in range(2):
            for zl in range(4):
                tile = [x[((yh * 8 + yl) * 2 + d0) * 32 + zl * 8 :][:8] for yl in range(8)]
                for i, piece in enumerate(turn(tile)):
                    pieces[zl, i % 4, i // 4, d0, yh] = piece
    x = jnp.concatenate([pieces[key] for key in sorted(pieces)], axis=0)
    x = attend(x, gain_ref[2:3, :], qkv_ref, out_ref)
    x = x.astype(BF16).astype(F32)
    normed = layer_norm(x, gain_ref[3:4, :])
    total = x
    for part in range(2):
        cols = slice(part * 1024, (part + 1) * 1024)
        hidden = jax.nn.gelu(dot(normed, up_ref[:, cols])).astype(BF16)
        total = total + dot(hidden, down_ref[cols, :])
    pieces = {key: total[8 * i : 8 * i + 8] for i, key in enumerate(sorted(pieces))}
    for zh in range(2):
        for yh in range(2):
            tiles = [
                turn([pieces[zl, w4, zh, d0, yh] for d0 in range(2) for w4 in range(4)])
                for zl in range(4)
            ]
            for y in range(2):
                for zl in range(4):
                    rows = jnp.concatenate(tiles[zl][4 * y : 4 * y + 4], axis=0)
                    at = ((yh * 2 + y) * 8 + zh * 4 + zl) * 32
                    y_ref[pl.ds(at, 32), :] = rows.astype(BF16)


def place_kernel(x_ref, y_ref):
    low = lax.broadcasted_iota(jnp.int32, (LINE, D), 0) % 8 < 4
    for hs in range(4):
        first = x_ref[hs // 2, :, hs % 2 * 2].reshape(LINE, D).astype(F32)
        second = x_ref[hs // 2, :, hs % 2 * 2 + 1].reshape(LINE, D).astype(F32)
        y_ref[0, hs] = jnp.where(low, first, pltpu.roll(second, 4, 0)).astype(BF16)
        y_ref[1, hs] = jnp.where(low, pltpu.roll(first, LINE - 4, 0), second).astype(BF16)


PARAMS = pltpu.CompilerParams(vmem_limit_bytes=40 * 1024 * 1024)
DISTANCES = (0, 7, 3, 5, 4, 2, 6, 1)
IN_HBM = pl.BlockSpec(memory_space=pltpu.HBM)
IN_VMEM = pl.BlockSpec(memory_space=pltpu.VMEM)


def weight_specs(layer):
    return [
        pl.BlockSpec((4, D), lambda *i: (0, 0)),
        pl.BlockSpec((None, D, 3 * D), lambda *i: (layer, 0, 0)),
        pl.BlockSpec((None, D, D), lambda *i: (layer, 0, 0)),
    ]


def whole(*shape):
    return pl.BlockSpec(shape, lambda *i: (0,) * len(shape))


def cost(nanoseconds):
    return pl.CostEstimate(flops=700_000 * nanoseconds, bytes_accessed=1 << 20, transcendentals=0)


def phase(kernel, shape, *operands, **options):
    return pl.pallas_call(
        kernel,
        in_specs=[IN_VMEM] * len(operands),
        out_specs=IN_VMEM,
        out_shape=jax.ShapeDtypeStruct(shape, BF16),
        compiler_params=PARAMS,
        **options,
    )(*operands)


def body(volume, qkv_weight, out_weight, norm_gain, up_weight, down_weight):
    weights = (norm_gain, qkv_weight, out_weight)
    half = (8, LINE, D)
    away, home, *first_weights = pl.pallas_call(
        width_away_kernel,
        in_specs=[IN_HBM] * 4,
        out_specs=[IN_VMEM] * 5,
        out_shape=[
            jax.ShapeDtypeStruct(half, BF16),
            jax.ShapeDtypeStruct(half, BF16),
            jax.ShapeDtypeStruct((4, D), F32),
            jax.ShapeDtypeStruct((D, 3 * D), BF16),
            jax.ShapeDtypeStruct((D, D), BF16),
        ],
        scratch_shapes=[pltpu.VMEM(half, BF16), pltpu.SemaphoreType.DMA((5,))],
        compiler_params=PARAMS,
        name="width_away",
    )(*[pltpu.with_memory_space_constraint(a, pltpu.HBM) for a in (volume, *weights)])
    away = lax.ppermute(away, "c", [(0, 1), (1, 0)])
    home = phase(width_home_kernel, half, home, *first_weights, name="width_home", cost_estimate=cost(3000))
    blocks = [jnp.stack([home[i], away[i]]) for i in range(8)]
    held = blocks[:1] + [
        lax.ppermute(blocks[i], ("zh", "zl"), [(z, (z + i) % 8) for z in range(8)]) for i in DISTANCES[1:]
    ]
    sent = pl.pallas_call(
        height_kernel,
        grid=(1,),
        in_specs=[whole(2, LINE, D)] * 8 + weight_specs(1),
        out_specs=whole(TOKENS, D),
        out_shape=jax.ShapeDtypeStruct((TOKENS, D), BF16),
        scratch_shapes=[pltpu.VMEM((8, 2, LINE, D), BF16)],
        compiler_params=PARAMS,
        name="height",
    )(*held, *weights)
    sent = sent.reshape(32, 32, D)
    held = lax.all_to_all(sent, ("y", "x", "c"), split_axis=0, concat_axis=0, tiled=True)
    sent = pl.pallas_call(
        depth_kernel,
        grid=(1,),
        in_specs=[whole(TOKENS, D)] + weight_specs(2) + [whole(D, FF), whole(FF, D)],
        out_specs=whole(TOKENS, D),
        out_shape=jax.ShapeDtypeStruct((TOKENS, D), BF16),
        compiler_params=PARAMS,
        name="depth",
    )(held.reshape(TOKENS, D), *weights, up_weight, down_weight)
    sent = sent.reshape(128, 8, D)
    held = lax.all_to_all(sent, ("y", "zh", "zl", "x"), split_axis=0, concat_axis=0, tiled=True)
    return pl.pallas_call(
        place_kernel,
        grid=(2,),
        in_specs=[pl.BlockSpec((2, 8, 4, 8, D), lambda i: (i, 0, 0, 0, 0))],
        out_specs=pl.BlockSpec((2, 4, LINE, D), lambda i: (0, i, 0, 0)),
        out_shape=jax.ShapeDtypeStruct((2, 8, LINE, D), BF16),
        compiler_params=PARAMS,
        name="place",
    )(held.reshape(4, 8, 4, 8, D))


def solution(mesh):
    fine = Mesh(mesh.devices.reshape(4, 4, 2, 4, 2), ("y", "x", "zh", "zl", "c"))
    return jax.shard_map(
        body,
        mesh=fine,
        in_specs=(P(("y", "x", "zh"), ("zl", "c"), None, None), P(), P(), P(), P(), P()),
        out_specs=P(("y", "x", "zh"), ("zl", "c"), None, None),
        check_vma=False,
    )
```

```python
import jax
import jax.numpy as jnp
from jax import lax
from jax.experimental import pallas as pl
from jax.experimental.pallas import tpu as pltpu
from jax.sharding import Mesh
from jax.sharding import PartitionSpec as P

D = 512
HEADS = 8
HEAD = 64
FF = 2048
LINE = 64
TOKENS = 1024
EPS = 1e-5
F32 = jnp.float32
BF16 = jnp.bfloat16


def layer_norm(x, gain):
    center = jnp.mean(x, axis=-1, keepdims=True)
    shifted = x - center
    spread = jnp.mean(shifted * shifted, axis=-1, keepdims=True)
    return (shifted * lax.rsqrt(spread + EPS) * gain).astype(BF16)


def dot(a, b):
    return jnp.dot(a, b, preferred_element_type=F32)


def softmax_top(scores, low):
    parts = []
    for half in range(2):
        s = scores[:, half * 128 : (half + 1) * 128]
        top_low = jnp.max(jnp.where(low, s, -jnp.inf), axis=-1, keepdims=True)
        top_high = jnp.max(jnp.where(low, -jnp.inf, s), axis=-1, keepdims=True)
        parts.append(jnp.exp(s - jnp.where(low, top_low, top_high)).astype(BF16))
    return jnp.concatenate(parts, axis=1)


def ones_block(crossed):
    row = lax.broadcasted_iota(jnp.int32, (256, 256), 0) // HEAD
    column = lax.broadcasted_iota(jnp.int32, (256, 256), 1) // HEAD
    if crossed:
        column = column + 1 - 2 * (column % 2)
    return jnp.where(row == column, 1.0, 0.0).astype(BF16)


def attend(x, gain, qkv_ref, out_ref, ready=None):
    n = x.shape[0] // LINE
    normed = layer_norm(x, gain)
    if ready:
        ready()
    q = (dot(normed, qkv_ref[:, :D]) * (HEAD**-0.5)).astype(BF16)
    k = dot(normed, qkv_ref[:, D : 2 * D]).astype(BF16).T
    v = dot(normed, qkv_ref[:, 2 * D :]).astype(BF16)
    low_row = lax.broadcasted_iota(jnp.int32, (1, 128), 1) < HEAD
    even = jnp.where(low_row, 1.0, 0.0).astype(BF16)
    odd = jnp.where(low_row, 0.0, 1.0).astype(BF16)
    low = lax.broadcasted_iota(jnp.int32, (LINE, 128), 1) < HEAD
    wide_low = lax.broadcasted_iota(jnp.int32, (LINE, 256), 1) % 128 < HEAD
    zero = jnp.zeros((128, 128), BF16)

    def diagonal(a, b):
        return jnp.concatenate(
            [jnp.concatenate([a, zero], axis=1), jnp.concatenate([zero, b], axis=1)], axis=0
        )

    exps = [[], []]
    mixed = [[], []]
    for pair in range(n // 2):
        at = 128 * pair
        a, b = slice(at, at + LINE), slice(at + LINE, at + 128)
        cells = []
        for p in range(4):
            c = slice(128 * p, 128 * p + 128)
            top = k[128 * p : 128 * p + 64, at : at + 128]
            bottom = k[128 * p + 64 : 128 * p + 128, at : at + 128]
            cells.append(
                (
                    (
                        q[a, c] * even + q[b, c] * odd,
                        jnp.concatenate([top * even, bottom * odd], axis=0),
                        jnp.concatenate([v[a, c] * even, v[b, c] * odd], axis=0),
                    ),
                    (
                        q[b, c] * even + q[a, c] * odd,
                        jnp.concatenate([top * odd, bottom * even], axis=0),
                        jnp.concatenate([v[a, c] * odd, v[b, c] * even], axis=0),
                    ),
                )
            )
        for g in range(2):
            for i in range(2):
                first, second = cells[2 * g][i], cells[2 * g + 1][i]
                scores = dot(
                    jnp.concatenate([first[0], second[0]], axis=1), diagonal(first[1], second[1])
                )
                e = softmax_top(scores, low)
                exps[i].append(e)
                mixed[i].append(dot(e, diagonal(first[2], second[2])))
    sums = [dot(jnp.concatenate(exps[i], axis=0), ones_block(i)) for i in range(2)]
    rows = []
    for pair in range(n // 2):
        of_a, of_b = [], []
        for g in range(2):
            at = 2 * pair + g
            r = [mixed[i][at] / sums[i][at * LINE : (at + 1) * LINE] for i in range(2)]
            of_a.append(jnp.where(wide_low, r[0], r[1]).astype(BF16))
            of_b.append(jnp.where(wide_low, r[1], r[0]).astype(BF16))
        rows += [jnp.concatenate(of_a, axis=1), jnp.concatenate(of_b, axis=1)]
    return x + dot(jnp.concatenate(rows, axis=0), out_ref[...])


def own_z():
    return lax.axis_index("zh") * 4 + lax.axis_index("zl")


def by_distance(y, y_ref):
    here = own_z()
    for z in range(8):
        pieces = [y[h * LINE + 8 * z :][:8] for h in range(8)]
        y_ref[lax.rem(z + 8 - here, 8)] = jnp.concatenate(pieces, axis=0).astype(BF16)


def width_away_kernel(
    x_hbm, gain_hbm, qkv_hbm, out_hbm, y_ref, home_ref, gain_ref, qkv_ref, out_ref, x_ref, sems
):
    core = lax.axis_index("c")
    copies = [
        pltpu.make_async_copy(source, target, sems.at[i])
        for i, (source, target) in enumerate(
            [
                (x_hbm.at[1 - core], x_ref),
                (gain_hbm, gain_ref),
                (qkv_hbm.at[0], qkv_ref),
                (out_hbm.at[0], out_ref),
                (x_hbm.at[core], home_ref),
            ]
        )
    ]
    for copy in copies:
        copy.start()
    def ready():
        for copy in copies[2:4]:
            copy.wait()

    for copy in copies[:2]:
        copy.wait()
    x = x_ref[...].reshape(8 * LINE, D).astype(F32)
    by_distance(attend(x, gain_ref[0:1, :], qkv_ref, out_ref, ready), y_ref)
    copies[4].wait()


def width_home_kernel(x_ref, gain_ref, qkv_ref, out_ref, y_ref):
    x = x_ref[...].reshape(8 * LINE, D).astype(F32)
    by_distance(attend(x, gain_ref[0:1, :], qkv_ref, out_ref), y_ref)


def turn(pieces):
    turned = jnp.swapaxes(jnp.concatenate(pieces, axis=0).reshape(8, 8, D), 0, 1)
    return [turned[i] for i in range(8)]


def height_kernel(*refs):
    *blocks, gain_ref, qkv_ref, out_ref, y_ref, x_ref = refs
    here, own_core = own_z(), lax.axis_index("c")
    for distance, block in zip(DISTANCES, blocks):
        for core in range(2):
            x_ref[lax.rem(here + 8 - distance, 8), lax.bitwise_xor(own_core, core)] = block[core]
    x = x_ref[...].astype(F32).reshape(2, LINE, 8, D)
    x = jnp.swapaxes(x, 1, 2).reshape(TOKENS, D)
    y = attend(x, gain_ref[1:2, :], qkv_ref, out_ref)
    for wsub in range(2):
        for c in range(2):
            tiles = [
                turn(
                    [
                        y[((zh * 2 + wsub) * 4 + w4) * LINE + (zl * 2 + c) * 8 :][:8]
                        for zh in range(2)
                        for w4 in range(4)
                    ]
                )
                for zl in range(4)
            ]
            for hs in range(8):
                rows = jnp.concatenate([tiles[zl][hs] for zl in range(4)], axis=0)
                y_ref[pl.ds((hs % 2 * 2 + wsub) * 256 + hs // 2 * 64 + c * 32, 32), :] = rows.astype(BF16)


def depth_kernel(x_ref, gain_ref, qkv_ref, out_ref, up_ref, down_ref, y_ref):
    x = x_ref[...].astype(F32)
    pieces = {}
    for yh in range(2):
        for d0 in range(2):
            for zl in range(4):
                tile = [x[(yl % 4 * 8 + (yh * 2 + yl // 4) * 2 + d0) * 32 + zl * 8 :][:8] for yl in range(8)]
                for i, piece in enumerate(turn(tile)):
                    pieces[zl, i % 4, i // 4, d0, yh] = piece
    x = jnp.concatenate([pieces[key] for key in sorted(pieces)], axis=0)
    x = attend(x, gain_ref[2:3, :], qkv_ref, out_ref)
    x = x.astype(BF16).astype(F32)
    normed = layer_norm(x, gain_ref[3:4, :])
    parts = []
    for at in range(0, TOKENS, 512):
        hidden = jax.nn.gelu(dot(normed[at : at + 512], up_ref[...])).astype(BF16)
        parts.append(x[at : at + 512] + dot(hidden, down_ref[...]))
    total = jnp.concatenate(parts, axis=0)
    pieces = {key: total[8 * i : 8 * i + 8] for i, key in enumerate(sorted(pieces))}
    for zh in range(2):
        for yh in range(2):
            tiles = [
                turn([pieces[zl, w4, zh, d0, yh] for d0 in range(2) for w4 in range(4)])
                for zl in range(4)
            ]
            for y in range(2):
                for zl in range(4):
                    rows = jnp.concatenate(tiles[zl][4 * y : 4 * y + 4], axis=0)
                    at = ((yh * 2 + y) * 8 + zh * 4 + zl) * 32
                    y_ref[pl.ds(at, 32), :] = rows.astype(BF16)


def place_kernel(x_ref, y_ref):
    low = lax.broadcasted_iota(jnp.int32, (LINE, D), 0) % 8 < 4
    for hs in range(4):
        first = x_ref[hs // 2, :, hs % 2 * 2].reshape(LINE, D).astype(F32)
        second = x_ref[hs // 2, :, hs % 2 * 2 + 1].reshape(LINE, D).astype(F32)
        y_ref[0, hs] = jnp.where(low, first, pltpu.roll(second, 4, 0)).astype(BF16)
        y_ref[1, hs] = jnp.where(low, pltpu.roll(first, LINE - 4, 0), second).astype(BF16)


PARAMS = pltpu.CompilerParams(vmem_limit_bytes=40 * 1024 * 1024)
DISTANCES = (0, 7, 3, 5, 4, 2, 6, 1)
IN_HBM = pl.BlockSpec(memory_space=pltpu.HBM)
IN_VMEM = pl.BlockSpec(memory_space=pltpu.VMEM)


def weight_specs(layer):
    return [
        pl.BlockSpec((4, D), lambda *i: (0, 0)),
        pl.BlockSpec((None, D, 3 * D), lambda *i: (layer, 0, 0)),
        pl.BlockSpec((None, D, D), lambda *i: (layer, 0, 0)),
    ]


def whole(*shape):
    return pl.BlockSpec(shape, lambda *i: (0,) * len(shape))


def cost(nanoseconds):
    return pl.CostEstimate(flops=700_000 * nanoseconds, bytes_accessed=1 << 20, transcendentals=0)


def phase(kernel, shape, *operands, **options):
    return pl.pallas_call(
        kernel,
        in_specs=[IN_VMEM] * len(operands),
        out_specs=IN_VMEM,
        out_shape=jax.ShapeDtypeStruct(shape, BF16),
        compiler_params=PARAMS,
        **options,
    )(*operands)


def body(volume, qkv_weight, out_weight, norm_gain, up_weight, down_weight):
    weights = (norm_gain, qkv_weight, out_weight)
    half = (8, LINE, D)
    away, home, *first_weights = pl.pallas_call(
        width_away_kernel,
        in_specs=[IN_HBM] * 4,
        out_specs=[IN_VMEM] * 5,
        out_shape=[
            jax.ShapeDtypeStruct(half, BF16),
            jax.ShapeDtypeStruct(half, BF16),
            jax.ShapeDtypeStruct((4, D), F32),
            jax.ShapeDtypeStruct((D, 3 * D), BF16),
            jax.ShapeDtypeStruct((D, D), BF16),
        ],
        scratch_shapes=[pltpu.VMEM(half, BF16), pltpu.SemaphoreType.DMA((5,))],
        compiler_params=PARAMS,
        name="width_away",
    )(*[pltpu.with_memory_space_constraint(a, pltpu.HBM) for a in (volume, *weights)])
    away = lax.ppermute(away, "c", [(0, 1), (1, 0)])
    home = phase(width_home_kernel, half, home, *first_weights, name="width_home", cost_estimate=cost(3000))
    blocks = [jnp.stack([home[i], away[i]]) for i in range(8)]
    held = blocks[:1] + [
        lax.ppermute(blocks[i], ("zh", "zl"), [(z, (z + i) % 8) for z in range(8)]) for i in DISTANCES[1:]
    ]
    sent = pl.pallas_call(
        height_kernel,
        grid=(1,),
        in_specs=[whole(2, LINE, D)] * 8 + weight_specs(1),
        out_specs=whole(TOKENS, D),
        out_shape=jax.ShapeDtypeStruct((TOKENS, D), BF16),
        scratch_shapes=[pltpu.VMEM((8, 2, LINE, D), BF16)],
        compiler_params=PARAMS,
        name="height",
    )(*held, *weights)
    sent = sent.reshape(32, 32, D)
    held = lax.all_to_all(sent, ("x", "y", "c"), split_axis=0, concat_axis=0, tiled=True)
    sent = pl.pallas_call(
        depth_kernel,
        grid=(1,),
        in_specs=[whole(TOKENS, D)] + weight_specs(2) + [whole(D, FF), whole(FF, D)],
        out_specs=whole(TOKENS, D),
        out_shape=jax.ShapeDtypeStruct((TOKENS, D), BF16),
        compiler_params=PARAMS,
        name="depth",
    )(held.reshape(TOKENS, D), *weights, up_weight, down_weight)
    sent = sent.reshape(128, 8, D)
    held = lax.all_to_all(sent, ("y", "zh", "zl", "x"), split_axis=0, concat_axis=0, tiled=True)
    return pl.pallas_call(
        place_kernel,
        grid=(2,),
        in_specs=[pl.BlockSpec((2, 8, 4, 8, D), lambda i: (i, 0, 0, 0, 0))],
        out_specs=pl.BlockSpec((2, 4, LINE, D), lambda i: (0, i, 0, 0)),
        out_shape=jax.ShapeDtypeStruct((2, 8, LINE, D), BF16),
        compiler_params=PARAMS,
        name="place",
    )(held.reshape(4, 8, 4, 8, D))


def solution(mesh):
    fine = Mesh(mesh.devices.reshape(4, 4, 2, 4, 2), ("y", "x", "zh", "zl", "c"))
    return jax.shard_map(
        body,
        mesh=fine,
        in_specs=(P(("y", "x", "zh"), ("zl", "c"), None, None), P(), P(), P(), P(), P()),
        out_specs=P(("y", "x", "zh"), ("zl", "c"), None, None),
        check_vma=False,
    )
```

```python
import jax
import jax.numpy as jnp
from jax import lax
from jax.experimental import pallas as pl
from jax.experimental.pallas import tpu as pltpu
from jax.sharding import Mesh
from jax.sharding import PartitionSpec as P

D = 512
HEADS = 8
HEAD = 64
FF = 2048
LINE = 64
TOKENS = 1024
EPS = 1e-5
F32 = jnp.float32
BF16 = jnp.bfloat16


def layer_norm(x, gain):
    center = jnp.mean(x, axis=-1, keepdims=True)
    shifted = x - center
    spread = jnp.mean(shifted * shifted, axis=-1, keepdims=True)
    return (shifted * lax.rsqrt(spread + EPS) * gain).astype(BF16)


def dot(a, b):
    return jnp.dot(a, b, preferred_element_type=F32)


def softmax_top(scores, low):
    parts = []
    for half in range(2):
        s = scores[:, half * 128 : (half + 1) * 128]
        top_low = jnp.max(jnp.where(low, s, -jnp.inf), axis=-1, keepdims=True)
        top_high = jnp.max(jnp.where(low, -jnp.inf, s), axis=-1, keepdims=True)
        parts.append(jnp.exp(s - jnp.where(low, top_low, top_high)).astype(BF16))
    return jnp.concatenate(parts, axis=1)


def ones_block(crossed):
    row = lax.broadcasted_iota(jnp.int32, (256, 256), 0) // HEAD
    column = lax.broadcasted_iota(jnp.int32, (256, 256), 1) // HEAD
    if crossed:
        column = column + 1 - 2 * (column % 2)
    return jnp.where(row == column, 1.0, 0.0).astype(BF16)


def attend(x, gain, qkv_ref, out_ref, ready=None):
    n = x.shape[0] // LINE
    normed = layer_norm(x, gain)
    if ready:
        ready()
    q = (dot(normed, qkv_ref[:, :D]) * (HEAD**-0.5)).astype(BF16)
    k = dot(normed, qkv_ref[:, D : 2 * D]).astype(BF16).T
    v = dot(normed, qkv_ref[:, 2 * D :]).astype(BF16)
    low_row = lax.broadcasted_iota(jnp.int32, (1, 128), 1) < HEAD
    even = jnp.where(low_row, 1.0, 0.0).astype(BF16)
    odd = jnp.where(low_row, 0.0, 1.0).astype(BF16)
    low = lax.broadcasted_iota(jnp.int32, (LINE, 128), 1) < HEAD
    wide_low = lax.broadcasted_iota(jnp.int32, (LINE, 256), 1) % 128 < HEAD
    zero = jnp.zeros((128, 128), BF16)

    def diagonal(a, b):
        return jnp.concatenate(
            [jnp.concatenate([a, zero], axis=1), jnp.concatenate([zero, b], axis=1)], axis=0
        )

    exps = [[], []]
    mixed = [[], []]
    for pair in range(n // 2):
        at = 128 * pair
        a, b = slice(at, at + LINE), slice(at + LINE, at + 128)
        cells = []
        for p in range(4):
            c = slice(128 * p, 128 * p + 128)
            top = k[128 * p : 128 * p + 64, at : at + 128]
            bottom = k[128 * p + 64 : 128 * p + 128, at : at + 128]
            cells.append(
                (
                    (
                        q[a, c] * even + q[b, c] * odd,
                        jnp.concatenate([top * even, bottom * odd], axis=0),
                        jnp.concatenate([v[a, c] * even, v[b, c] * odd], axis=0),
                    ),
                    (
                        q[b, c] * even + q[a, c] * odd,
                        jnp.concatenate([top * odd, bottom * even], axis=0),
                        jnp.concatenate([v[a, c] * odd, v[b, c] * even], axis=0),
                    ),
                )
            )
        for g in range(2):
            for i in range(2):
                first, second = cells[2 * g][i], cells[2 * g + 1][i]
                scores = dot(
                    jnp.concatenate([first[0], second[0]], axis=1), diagonal(first[1], second[1])
                )
                e = softmax_top(scores, low)
                exps[i].append(e)
                mixed[i].append(dot(e, diagonal(first[2], second[2])))
    sums = [dot(jnp.concatenate(exps[i], axis=0), ones_block(i)) for i in range(2)]
    rows = []
    for pair in range(n // 2):
        of_a, of_b = [], []
        for g in range(2):
            at = 2 * pair + g
            r = [mixed[i][at] / sums[i][at * LINE : (at + 1) * LINE] for i in range(2)]
            of_a.append(jnp.where(wide_low, r[0], r[1]).astype(BF16))
            of_b.append(jnp.where(wide_low, r[1], r[0]).astype(BF16))
        rows += [jnp.concatenate(of_a, axis=1), jnp.concatenate(of_b, axis=1)]
    return x + dot(jnp.concatenate(rows, axis=0), out_ref[...])


def own_z():
    return lax.axis_index("zh") * 4 + lax.axis_index("zl")


def by_distance(y, y_ref):
    here = own_z()
    for z in range(8):
        pieces = [y[h * LINE + 8 * z :][:8] for h in range(8)]
        y_ref[lax.rem(z + 8 - here, 8)] = jnp.concatenate(pieces, axis=0).astype(BF16)


def width_away_kernel(
    x_hbm, gain_hbm, qkv_hbm, out_hbm, y_ref, home_ref, gain_ref, qkv_ref, out_ref, x_ref, sems
):
    core = lax.axis_index("c")
    copies = [
        pltpu.make_async_copy(source, target, sems.at[i])
        for i, (source, target) in enumerate(
            [
                (x_hbm.at[1 - core], x_ref),
                (gain_hbm, gain_ref),
                (qkv_hbm.at[0], qkv_ref),
                (out_hbm.at[0], out_ref),
                (x_hbm.at[core], home_ref),
            ]
        )
    ]
    for copy in copies:
        copy.start()
    def ready():
        for copy in copies[2:4]:
            copy.wait()

    for copy in copies[:2]:
        copy.wait()
    x = x_ref[...].reshape(8 * LINE, D).astype(F32)
    by_distance(attend(x, gain_ref[0:1, :], qkv_ref, out_ref, ready), y_ref)
    copies[4].wait()


def width_home_kernel(x_ref, gain_ref, qkv_ref, out_ref, y_ref):
    x = x_ref[...].reshape(8 * LINE, D).astype(F32)
    by_distance(attend(x, gain_ref[0:1, :], qkv_ref, out_ref), y_ref)


def turn(pieces):
    turned = jnp.swapaxes(jnp.concatenate(pieces, axis=0).reshape(8, 8, D), 0, 1)
    return [turned[i] for i in range(8)]


def height_kernel(*refs):
    *blocks, gain_ref, qkv_ref, out_ref, y_ref, x_ref = refs
    here, own_core = own_z(), lax.axis_index("c")
    for distance, block in zip(DISTANCES, blocks):
        for core in range(2):
            x_ref[lax.rem(here + 8 - distance, 8), lax.bitwise_xor(own_core, core)] = block[core]
    x = x_ref[...].astype(F32).reshape(2, LINE, 8, D)
    x = jnp.swapaxes(x, 1, 2).reshape(TOKENS, D)
    y = attend(x, gain_ref[1:2, :], qkv_ref, out_ref)
    for wsub in range(2):
        for c in range(2):
            tiles = [
                turn(
                    [
                        y[((zh * 2 + wsub) * 4 + w4) * LINE + (zl * 2 + c) * 8 :][:8]
                        for zh in range(2)
                        for w4 in range(4)
                    ]
                )
                for zl in range(4)
            ]
            for hs in range(8):
                rows = jnp.concatenate([tiles[zl][hs] for zl in range(4)], axis=0)
                y_ref[pl.ds((hs % 2 * 2 + wsub) * 256 + hs // 2 * 64 + c * 32, 32), :] = rows.astype(BF16)


def depth_kernel(x_ref, gain_ref, qkv_ref, out_ref, up_ref, down_ref, y_ref):
    x = x_ref[...].astype(F32)
    pieces = {}
    for yh in range(2):
        for d0 in range(2):
            for zl in range(4):
                tile = [x[(yl % 4 * 8 + (yh * 2 + yl // 4) * 2 + d0) * 32 + zl * 8 :][:8] for yl in range(8)]
                for i, piece in enumerate(turn(tile)):
                    pieces[zl, i % 4, i // 4, d0, yh] = piece
    x = jnp.concatenate([pieces[key] for key in sorted(pieces)], axis=0)
    x = attend(x, gain_ref[2:3, :], qkv_ref, out_ref)
    x = x.astype(BF16).astype(F32)
    normed = layer_norm(x, gain_ref[3:4, :])
    parts = []
    for at in range(0, TOKENS, 512):
        hidden = jax.nn.gelu(dot(normed[at : at + 512], up_ref[...])).astype(BF16)
        parts.append(x[at : at + 512] + dot(hidden, down_ref[...]))
    total = jnp.concatenate(parts, axis=0)
    pieces = {key: total[8 * i : 8 * i + 8] for i, key in enumerate(sorted(pieces))}
    for zh in range(2):
        for yh in range(2):
            tiles = [
                turn([pieces[zl, w4, zh, d0, yh] for d0 in range(2) for w4 in range(4)])
                for zl in range(4)
            ]
            for y in range(2):
                for zl in range(4):
                    rows = jnp.concatenate(tiles[zl][4 * y : 4 * y + 4], axis=0)
                    at = ((yh * 2 + y) * 8 + Z_PLACE[zh * 4 + zl]) * 32
                    y_ref[pl.ds(at, 32), :] = rows.astype(BF16)


def place_kernel(x_ref, y_ref):
    low = lax.broadcasted_iota(jnp.int32, (LINE, D), 0) % 8 < 4
    for hs in range(4):
        first, second = [
            jnp.concatenate(
                [x_ref[hs // 2, place, hs % 2 * 2 + wsub].astype(F32) for place in Z_PLACE], axis=0
            )
            for wsub in range(2)
        ]
        y_ref[0, hs] = jnp.where(low, first, pltpu.roll(second, 4, 0)).astype(BF16)
        y_ref[1, hs] = jnp.where(low, pltpu.roll(first, LINE - 4, 0), second).astype(BF16)


PARAMS = pltpu.CompilerParams(vmem_limit_bytes=40 * 1024 * 1024)
Z_PLACE = [3 * z % 8 for z in range(8)]
GROUPS = [
    [((y * 4 + x) * 8 + z) * 2 + core for y in range(4) for z in Z_PLACE for x in range(4)] for core in range(2)
]
DISTANCES = (0, 1, 5, 3, 4, 6, 2, 7)
IN_HBM = pl.BlockSpec(memory_space=pltpu.HBM)
IN_VMEM = pl.BlockSpec(memory_space=pltpu.VMEM)


def weight_specs(layer):
    return [
        pl.BlockSpec((4, D), lambda *i: (0, 0)),
        pl.BlockSpec((None, D, 3 * D), lambda *i: (layer, 0, 0)),
        pl.BlockSpec((None, D, D), lambda *i: (layer, 0, 0)),
    ]


def whole(*shape):
    return pl.BlockSpec(shape, lambda *i: (0,) * len(shape))


def cost(nanoseconds):
    return pl.CostEstimate(flops=700_000 * nanoseconds, bytes_accessed=1 << 20, transcendentals=0)


def phase(kernel, shape, *operands, **options):
    return pl.pallas_call(
        kernel,
        in_specs=[IN_VMEM] * len(operands),
        out_specs=IN_VMEM,
        out_shape=jax.ShapeDtypeStruct(shape, BF16),
        compiler_params=PARAMS,
        **options,
    )(*operands)


def body(volume, qkv_weight, out_weight, norm_gain, up_weight, down_weight):
    weights = (norm_gain, qkv_weight, out_weight)
    half = (8, LINE, D)
    away, home, *first_weights = pl.pallas_call(
        width_away_kernel,
        in_specs=[IN_HBM] * 4,
        out_specs=[IN_VMEM] * 5,
        out_shape=[
            jax.ShapeDtypeStruct(half, BF16),
            jax.ShapeDtypeStruct(half, BF16),
            jax.ShapeDtypeStruct((4, D), F32),
            jax.ShapeDtypeStruct((D, 3 * D), BF16),
            jax.ShapeDtypeStruct((D, D), BF16),
        ],
        scratch_shapes=[pltpu.VMEM(half, BF16), pltpu.SemaphoreType.DMA((5,))],
        compiler_params=PARAMS,
        name="width_away",
    )(*[pltpu.with_memory_space_constraint(a, pltpu.HBM) for a in (volume, *weights)])
    away = lax.ppermute(away, "c", [(0, 1), (1, 0)])
    home = phase(width_home_kernel, half, home, *first_weights, name="width_home", cost_estimate=cost(3000))
    blocks = [jnp.stack([home[i], away[i]]) for i in range(8)]
    held = blocks[:1] + [
        lax.ppermute(blocks[i], ("zh", "zl"), [(z, (z + i) % 8) for z in range(8)]) for i in DISTANCES[1:]
    ]
    sent = pl.pallas_call(
        height_kernel,
        grid=(1,),
        in_specs=[whole(2, LINE, D)] * 8 + weight_specs(1),
        out_specs=whole(TOKENS, D),
        out_shape=jax.ShapeDtypeStruct((TOKENS, D), BF16),
        scratch_shapes=[pltpu.VMEM((8, 2, LINE, D), BF16)],
        compiler_params=PARAMS,
        name="height",
    )(*held, *weights)
    sent = sent.reshape(32, 32, D)
    held = lax.all_to_all(sent, ("x", "y", "c"), split_axis=0, concat_axis=0, tiled=True)
    sent = pl.pallas_call(
        depth_kernel,
        grid=(1,),
        in_specs=[whole(TOKENS, D)] + weight_specs(2) + [whole(D, FF), whole(FF, D)],
        out_specs=whole(TOKENS, D),
        out_shape=jax.ShapeDtypeStruct((TOKENS, D), BF16),
        compiler_params=PARAMS,
        name="depth",
    )(held.reshape(TOKENS, D), *weights, up_weight, down_weight)
    sent = sent.reshape(128, 8, D)
    held = lax.all_to_all(
        sent, ("y", "x", "zh", "zl", "c"), split_axis=0, concat_axis=0, tiled=True, axis_index_groups=GROUPS
    )
    return pl.pallas_call(
        place_kernel,
        grid=(2,),
        in_specs=[pl.BlockSpec((2, 8, 4, 8, D), lambda i: (i, 0, 0, 0, 0))],
        out_specs=pl.BlockSpec((2, 4, LINE, D), lambda i: (0, i, 0, 0)),
        out_shape=jax.ShapeDtypeStruct((2, 8, LINE, D), BF16),
        compiler_params=PARAMS,
        name="place",
    )(held.reshape(4, 8, 4, 8, D))


def solution(mesh):
    fine = Mesh(mesh.devices.reshape(4, 4, 2, 4, 2), ("y", "x", "zh", "zl", "c"))
    return jax.shard_map(
        body,
        mesh=fine,
        in_specs=(P(("y", "x", "zh"), ("zl", "c"), None, None), P(), P(), P(), P(), P()),
        out_specs=P(("y", "x", "zh"), ("zl", "c"), None, None),
        check_vma=False,
    )
```
